512 devices in a mesh: seq: 16 (over y, core), head: 32 (over x, z).
Axes of the slice: x: 4, y: 8, z: 8, core: 2. Of those that a mesh axis runs over, the one named last changes fastest.
Arguments:
- x_raw: bfloat16 [4096, 16384], P('seq', 'head'), may hold values from -10 to 10
- bc_raw: bfloat16 [4096, 4096], P('seq'), may hold values from -10 to 10
- z_raw: bfloat16 [4096, 16384], P('seq', 'head'), may hold values from -3000 to 3000
- x_kernel: float32 [4, 16384], P(None, 'head'), may hold values from -3 to 3
- bc_kernel: float32 [4, 4096], replicated, may hold values from -3 to 3
- x_offset: float32 [16384], P('head'), may hold values from -1.6 to -0.4
- bc_offset: float32 [4096], replicated, may hold values from -1.6 to -0.4
- dt_raw: float32 [4096, 256], P('seq', 'head'), may hold values from -1.5 to 9.5
- dt_bias: float32 [256], P('head'), may hold values from -7 to -2.5
- a_log: float32 [256], P('head'), may hold values from -5 to 3.5
- d_skip: float32 [256], P('head'), may hold values from 0.5 to 1.5
- norm_gain: float32 [16384], P('head'), may hold values from 0.25 to 1.75
- out_weight: bfloat16 [16384, 8192], P('head', 'seq'), may hold values from -0.09375 to 0.09375
Outputs:
- mixed: bfloat16 [4096, 8192], P('seq', 'head')
The draws below stay inside these ranges and needn't reach their ends.
All inputs are finite; a program needn't handle non-finite values.
Results may differ from the reference program's by a relative error of at most 0.034.
Values may be sent and summed in bfloat16 or wider, within the bound.
A program may use at most 64 MiB of HBM per device.

```python
import jax
import jax.numpy as jnp
from jax import lax

D = 8192
P_SIZE = 64
N = 256
HPG = 32
KW = 4
SPAN = 256
HEAD_DEV = 8
HEADS = 256
GROUPS = 8
TOK_DEV = 256
SLAB_TOKENS = 4096
N_HEAD = 32


def head_rates(key, share):
    random_keys = jax.random.split(key, 4)
    slow_heads = jax.random.randint(random_keys[0], (HEADS,), 0, 100) < share
    step_target = jnp.where(slow_heads, 0.002, 0.04) * jnp.exp(jax.random.uniform(random_keys[1], (HEADS,), jnp.float32, -0.3, 0.3))
    chain_log = jax.random.uniform(random_keys[2], (HEADS,), jnp.float32, 0.7, 1.4)
    fast_decay = jnp.exp(jax.random.uniform(random_keys[3], (HEADS,), jnp.float32, -0.3, 0.3)) / min(40.0, SPAN / 4.0)
    decay_step = jnp.where(slow_heads, chain_log / SLAB_TOKENS, fast_decay)
    return (step_target, decay_step / step_target)


def draw_x_raw(key, part):
    key = jax.random.fold_in(key, 14)
    random_keys = jax.random.split(key, 2)
    width = HEADS * P_SIZE
    block_len = SPAN // 2
    block_count = SLAB_TOKENS // block_len
    tokenwise = jnp.clip(jax.random.normal(random_keys[0], (SLAB_TOKENS, width), jnp.float32), -5.0, 5.0)
    blockwise = jnp.clip(jax.random.normal(random_keys[1], (block_count, width), jnp.float32), -5.0, 5.0)
    return (tokenwise + jnp.repeat(blockwise, block_len, axis=0)).astype(jnp.bfloat16)


def draw_bc_raw(key, part):
    key = jax.random.fold_in(key, 15)
    random_keys = jax.random.split(key, 2)
    width = 2 * GROUPS * N
    block_len = SPAN // 2
    block_count = SLAB_TOKENS // block_len
    tokenwise = jnp.clip(jax.random.normal(random_keys[0], (SLAB_TOKENS, width), jnp.float32), -5.0, 5.0)
    blockwise = jnp.clip(jax.random.normal(random_keys[1], (block_count, width), jnp.float32), -5.0, 5.0)
    return (tokenwise + jnp.repeat(blockwise, block_len, axis=0)).astype(jnp.bfloat16)


def draw_z_raw(key, part):
    key = jax.random.fold_in(key, 11)
    random_keys = jax.random.split(key, 3)
    chan_total = HEADS * P_SIZE
    group_width = HPG * P_SIZE
    positions = (jnp.arange(chan_total) % group_width).astype(jnp.float32) / group_width
    base = jnp.clip(jax.random.normal(random_keys[0], (SLAB_TOKENS, chan_total), jnp.float32), -5.0, 5.0)
    jitter = jax.random.uniform(random_keys[1], (chan_total,), jnp.float32, -0.08, 0.08)
    col_scale = 10.0 ** (positions + jitter)
    row_scale = 10.0 ** jax.random.uniform(random_keys[2], (SLAB_TOKENS, 1), jnp.float32)
    return (base * col_scale[None, :] * row_scale).astype(jnp.bfloat16)


def draw_dt_bias(key, part):
    share = 50
    step_target, decay_scale = head_rates(key, share)
    return jnp.log(jnp.expm1(step_target))


def draw_a_log(key, part):
    share = 50
    step_target, decay_scale = head_rates(key, share)
    return jnp.log(decay_scale)


def draw_dt_raw(key, part):
    key = jax.random.fold_in(key, 13)
    random_keys = jax.random.split(key, 3)
    base = jnp.clip(0.3 * jax.random.normal(random_keys[0], (SLAB_TOKENS, HEADS), jnp.float32), -1.0, 1.0)
    block_shift = jax.random.uniform(random_keys[1], (SLAB_TOKENS // TOK_DEV, HEADS), jnp.float32, -0.5, 0.5)
    block_shift = jnp.repeat(block_shift, TOK_DEV, axis=0)
    gathered_rows = jax.random.randint(random_keys[2], (3,), 0, SLAB_TOKENS)
    matched_entry = jnp.any(jnp.arange(SLAB_TOKENS)[:, None] == gathered_rows[None, :], axis=1)
    return base + block_shift + jnp.where(matched_entry, 8.0, 0.0)[:, None]


def raised(result, own_key, source, target, parts, factor):
    owner, partner = [(jnp.arange(result.shape[axis_at]) // (result.shape[axis_at] // parts)).reshape([-1 if axis == axis_at else 1 for axis in range(result.ndim)]) for axis_at in (source, target)]
    chosen = jax.random.permutation(own_key, parts)[partner]
    strong = (owner == chosen) | (owner == (partner + parts // 2) % parts)
    return jnp.where(strong, factor * result, result)


def block_levels(own_key, dims, cuts, least, largest):
    def one(axis_at, shards_of):
        steps = jax.random.uniform(jax.random.fold_in(jax.random.fold_in(own_key, 6), axis_at), (shards_of,), jnp.float32, least / len(cuts), largest / len(cuts))
        return jnp.repeat(jnp.exp(steps), dims[axis_at] // shards_of).reshape((-1,) + (1,) * (len(dims) - axis_at - 1))

    factor_of = one(*cuts[0])
    for cut in cuts[1:]:
        factor_of = factor_of * one(*cut)
    return factor_of


def normal_values(own_key, dims, spread, reach, cuts=(), held_as=jnp.bfloat16):
    array = spread * jax.random.normal(own_key, dims, jnp.float32)
    if cuts:
        array = array * block_levels(own_key, dims, cuts, -0.22, 0.18)
    return jnp.clip(array, -reach, reach).astype(held_as)


def gaussian_with(key, extent, scale, reach, cuts, heavy, held_as=jnp.bfloat16):
    array = scale * jax.random.normal(key, extent, jnp.float32)
    if cuts:
        array = array * block_levels(key, extent, cuts, -0.22, 0.18)
    return jnp.clip(raised(array, jax.random.fold_in(key, 3), *heavy), -reach, reach).astype(held_as)


def setup_inputs(seed: int = 0) -> dict:
    key_list = jax.random.split(jax.random.key(seed), 14)
    x_raw = draw_x_raw(jax.random.fold_in(key_list[13], 71), 0)
    bc_raw = draw_bc_raw(jax.random.fold_in(key_list[13], 71), 0)
    z_raw = draw_z_raw(jax.random.fold_in(key_list[13], 71), 0)
    x_kernel = normal_values(key_list[3], (KW, HEADS * P_SIZE), KW ** -0.5, 3.0, ((1, 32),), jnp.float32)
    bc_kernel = normal_values(key_list[4], (KW, 2 * GROUPS * N), KW ** -0.5, 3.0, (), jnp.float32)
    x_offset = jnp.clip(-1.6 + 1.2 * jax.random.uniform(key_list[5], (HEADS * P_SIZE,), jnp.float32) ** block_levels(key_list[5], (HEADS * P_SIZE,), ((0, 32),), -0.2, 0.2), -1.6, -0.4)
    bc_offset = jnp.clip(jax.random.uniform(key_list[6], (2 * GROUPS * N,), jnp.float32, -1.6, -0.4), -1.6, -0.4)
    dt_raw = draw_dt_raw(jax.random.fold_in(key_list[13], 71), 0)
    dt_bias = draw_dt_bias(jax.random.fold_in(key_list[13], 71), 0)
    a_log = draw_a_log(jax.random.fold_in(key_list[13], 71), 0)
    d_skip = jnp.clip(0.5 + 1.0 * jax.random.uniform(key_list[10], (HEADS,), jnp.float32) ** block_levels(key_list[10], (HEADS,), ((0, 32),), -0.2, 0.2), 0.5, 1.5)
    norm_gain = jnp.clip(1.0 + 0.15 * jax.random.normal(key_list[11], (HEADS * P_SIZE,), jnp.float32), 0.25, 1.75)
    out_weight = gaussian_with(key_list[12], (HEADS * P_SIZE, D), (HEADS * P_SIZE) ** -0.5, 0.09375, ((0, 32), (1, 16)), (0, 1, 32, 2.75))
    return dict(x_raw=x_raw, bc_raw=bc_raw, z_raw=z_raw, x_kernel=x_kernel, bc_kernel=bc_kernel, x_offset=x_offset, bc_offset=bc_offset, dt_raw=dt_raw, dt_bias=dt_bias, a_log=a_log, d_skip=d_skip, norm_gain=norm_gain, out_weight=out_weight)


norm_eps = 1e-05

def causal_conv(raw, prefix, kernel, offset):
    taps = kernel.shape[0]
    length = raw.shape[0]
    padded = jnp.concatenate([prefix.astype(jnp.float32), raw.astype(jnp.float32)], axis=0)
    running = jnp.zeros((length, raw.shape[1]), jnp.float32) + offset.astype(jnp.float32)[None, :]
    for k in range(taps):
        running = running + kernel[k].astype(jnp.float32)[None, :] * padded[k:k + length]
    return jax.nn.silu(running).astype(jnp.bfloat16)

def reference(x_raw, bc_raw, z_raw, x_kernel, bc_kernel, x_offset, bc_offset, dt_raw, dt_bias, a_log, d_skip, norm_gain, out_weight):
    head_total = HEAD_DEV * N_HEAD
    groups = head_total // HPG
    tokens = x_raw.shape[0]
    span_count = tokens // SPAN
    taps = x_kernel.shape[0]
    x_conv = causal_conv(x_raw, jnp.zeros((taps - 1, x_raw.shape[1]), jnp.float32), x_kernel, x_offset)
    bc_conv = causal_conv(bc_raw, jnp.zeros((taps - 1, bc_raw.shape[1]), jnp.float32), bc_kernel, bc_offset)
    step_size = jax.nn.softplus(dt_raw + dt_bias[None, :])
    a_rate = -jnp.exp(a_log)
    x_spans = x_conv.reshape(span_count, SPAN, head_total, P_SIZE)
    b_spans = bc_conv[:, :groups * N].reshape(span_count, SPAN, groups, N)
    c_spans = bc_conv[:, groups * N:].reshape(span_count, SPAN, groups, N)
    dt_spans = step_size.reshape(span_count, SPAN, head_total)
    positions = jnp.arange(SPAN)
    causal_mask = (positions[:, None] >= positions[None, :])[None]

    def one_span(carried, pieces):
        x_block, b_block, c_block, dt_block = pieces
        cum_logs = jnp.cumsum(dt_block * a_rate[None, :], axis=0)
        pair_gap = cum_logs.T[:, :, None] - cum_logs.T[:, None, :]
        decay_mask = jnp.where(causal_mask, jnp.exp(jnp.where(causal_mask, pair_gap, 0.0)), 0.0)
        inner_cb = jnp.einsum('tgn,sgn->gts', c_block.astype(jnp.float32), b_block.astype(jnp.float32))
        inner_cb = jnp.repeat(inner_cb, HPG, axis=0)
        mixing = (decay_mask * inner_cb * dt_block.T[:, None, :]).astype(jnp.bfloat16)
        x_float = x_block.astype(jnp.float32)
        y_diag = jnp.einsum('hts,shp->thp', mixing.astype(jnp.float32), x_float)
        y_off = jnp.einsum('tgn,gkpn->tgkp', c_block.astype(jnp.float32), carried.reshape(groups, HPG, P_SIZE, N), precision=lax.Precision.HIGHEST)
        y_off = y_off.reshape(SPAN, head_total, P_SIZE) * jnp.exp(cum_logs)[:, :, None]
        y_block = y_diag + y_off + d_skip[None, :, None] * x_float
        end_weight = jnp.exp(cum_logs[-1][None, :] - cum_logs) * dt_block
        input_weighted = (x_float * end_weight[:, :, None]).astype(jnp.bfloat16)
        local_state = jnp.einsum('tgkp,tgn->gkpn', input_weighted.astype(jnp.float32).reshape(SPAN, groups, HPG, P_SIZE), b_block.astype(jnp.float32))
        carried = jnp.exp(cum_logs[-1])[:, None, None] * carried + local_state.reshape(head_total, P_SIZE, N)
        return (carried, y_block)
    zero_state = jnp.zeros((head_total, P_SIZE, N), jnp.float32)
    _, y_blocks = lax.scan(one_span, zero_state, (x_spans, b_spans, c_spans, dt_spans))
    y_all = y_blocks.reshape(tokens, head_total * P_SIZE)
    gated = y_all * jax.nn.silu(z_raw.astype(jnp.float32))
    grouped = gated.reshape(tokens, groups, HPG * P_SIZE)
    inv_rms = lax.rsqrt(lax.optimization_barrier(jnp.mean(grouped * grouped, axis=2, keepdims=True)) + norm_eps)
    normed = ((grouped * inv_rms).reshape(tokens, head_total * P_SIZE) * norm_gain[None, :]).astype(jnp.bfloat16)
    chan_width = HEAD_DEV * P_SIZE
    normalized_blocks = normed.reshape(tokens, N_HEAD, chan_width).transpose(1, 0, 2)
    weight_blocks = out_weight.reshape(N_HEAD, chan_width, out_weight.shape[1])

    def add_block(running, block_pair):
        partial_value = jnp.dot(block_pair[0], block_pair[1], preferred_element_type=jnp.float32).astype(jnp.bfloat16)
        partial_value = lax.optimization_barrier(partial_value)
        return (running + partial_value.astype(jnp.float32), None)
    summed, _ = lax.scan(add_block, jnp.zeros((tokens, out_weight.shape[1]), jnp.float32), (normalized_blocks, weight_blocks))
    return summed.astype(jnp.bfloat16)
```

```python
import jax
import jax.numpy as jnp
from jax import lax
from jax.experimental import pallas as pl
from jax.experimental.pallas import tpu as pltpu
from jax.sharding import PartitionSpec as P

P_SIZE = 64
N = 256
TOK = 256
CH = 512
HEADS_DEV = 8
NY, NX, NZ = 8, 4, 8
SLOTS = 8
norm_eps = 1e-05
MESH = pl.DeviceIdType.MESH
HI = lax.Precision.HIGHEST
f32 = jnp.float32
bf16 = jnp.bfloat16


def dot(a, b, dims, precision=None):
    return lax.dot_general(a, b, (dims, ((), ())), precision=precision, preferred_element_type=f32)


def kernel(
    x_hbm,
    bc_hbm,
    z_hbm,
    xk_ref,
    bck_ref,
    xo_ref,
    bco_ref,
    dt_ref,
    dtb_ref,
    alog_ref,
    dsk_ref,
    gain_ref,
    w_hbm,
    o_ref,
    xbc,
    zb,
    wb,
    load_sem,
    halo,
    raw,
    conv,
    cum,
    dts,
    rows,
    ybase,
    state,
    statebf,
    sibstate,
    dec,
    decall,
    total,
    gath,
    entout,
    entchip,
    entsend,
    ent,
    sq,
    slot_in,
    part,
    xlong,
    xshort,
    strip,
    zin,
    fin,
    out,
    scan_send,
    scan_recv,
    y_send,
    y_recv,
    c_send,
    c_recv,
    x_send,
    x_recv,
    z_send,
    z_recv,
    f_send,
    f_recv,
):
    seq = lax.axis_index("seq")
    head = lax.axis_index("head")
    Y, C = seq // 2, seq % 2
    X, Z = head // NZ, head % NZ
    group = head // 4
    other = 1 - C

    def at(y, c, x, z):
        return (y * 2 + c, x * NZ + z)

    sibling = at(Y, other, X, Z)
    y_next, y_prev = lax.rem(Y + 1, NY), lax.rem(Y + NY - 1, NY)
    after = (lax.rem(seq + 1, 16), head)
    before = (lax.rem(seq + 15, 16), head)
    cross = at(lax.rem(Y + NY - 1 + 2 * C, NY), other, X, Z)
    sigma = 1 - 2 * C
    x_fwd = at(Y, C, lax.rem(X + NX + sigma, NX), Z)
    x_back = at(Y, C, lax.rem(X + NX - sigma, NX), Z)

    def y_at(k):
        return at(lax.rem(Y + k, NY), C, X, Z)

    def z_at(k):
        return at(Y, C, X, lax.rem(Z + k, NZ))

    owner_c = X // 2
    owner_x = Y // 2
    owner_z = 4 * lax.rem(Y, 2) + 2 * C

    def same(a, b):
        return jnp.logical_and(a[0] == b[0], a[1] == b[1])

    me = (seq, head)

    barrier = pltpu.get_barrier_semaphore()

    def greet(device):
        pl.semaphore_signal(barrier, inc=1, device_id=device, device_id_type=MESH)

    greet(sibling)
    greet(cross)
    for k in range(1, NY):
        greet(y_at(k))
    for k in range(1, NZ):
        greet(z_at(k))
    greet(x_fwd)
    greet(x_back)
    src_y = 2 * X + Z // 4
    src_c = lax.rem(Z // 2, 2)
    for dx in range(2):

        def greet_source(z, carry, dx=dx):
            device = at(src_y, src_c, 2 * C + dx, z)

            @pl.when(jnp.logical_not(same(device, me)))
            def _():
                greet(device)

            return carry

        lax.fori_loop(0, NZ, greet_source, 0)
    stays = jnp.logical_and(
        jnp.logical_and(owner_x == X, owner_c == C), Z // 2 == owner_z // 2
    ).astype(jnp.int32)

    def load(i, src, dst):
        copy = pltpu.make_async_copy(src, dst, load_sem.at[i])
        copy.start()
        return copy

    b_start = pl.multiple_of(group * N, N)
    c_start = pl.multiple_of(8 * N + group * N, N)
    loads = [
        load(0, x_hbm, xbc.at[:, pl.ds(0, CH)]),
        load(1, bc_hbm.at[:, pl.ds(b_start, N)], xbc.at[:, pl.ds(CH, N)]),
        load(2, bc_hbm.at[:, pl.ds(c_start, N)], xbc.at[:, pl.ds(CH + N, N)]),
    ]
    z_load = load(3, z_hbm, zb)
    w_load = load(4, w_hbm, wb)

    pos_t = lax.broadcasted_iota(jnp.int32, (TOK, TOK), 0)
    pos_s = lax.broadcasted_iota(jnp.int32, (TOK, TOK), 1)
    causal = pos_t >= pos_s
    step_in = dt_ref[...] + dtb_ref[...]
    step = jnp.maximum(step_in, 0.0) + jnp.log1p(jnp.exp(-jnp.abs(step_in)))
    log_step = step * -jnp.exp(alog_ref[...])
    cum_cols = dot(causal.astype(f32), log_step, ((1,), (0,)), HI)
    cum[...] = cum_cols
    dts[...] = step
    eye = (pos_t == pos_s).astype(f32)
    rows[0:8, :] = dot(cum_cols, eye, ((0,), (0,)), HI)
    rows[8:16, :] = dot(step, eye, ((0,), (0,)), HI)
    last_cols = cum_cols[TOK - 1 : TOK, :]
    dec[0] = jnp.broadcast_to(jnp.exp(rows[0:8, TOK - 1 : TOK]), (8, TOK))
    spread = (
        lax.broadcasted_iota(jnp.int32, (HEADS_DEV, CH), 1) // P_SIZE
        == lax.broadcasted_iota(jnp.int32, (HEADS_DEV, CH), 0)
    ).astype(f32)
    end_weight = dot(jnp.exp(last_cols - cum_cols) * step, spread, ((1,), (0,)), HI)

    for copy in loads:
        copy.wait()
    pl.semaphore_wait(barrier, 2 + (NY - 1) + (NZ - 1) + 2 + 16 - stays)

    def remote(src, dst, send, recv, device):
        return pltpu.make_async_remote_copy(
            src_ref=src, dst_ref=dst, send_sem=send, recv_sem=recv, device_id=device, device_id_type=MESH
        )

    def arrived(ref, sem):
        pltpu.make_async_copy(ref, ref, sem).wait()

    halo_copy = remote(xbc.at[pl.ds(TOK - 16, 16)], halo, scan_send.at[0], scan_recv.at[0], after)
    halo_copy.start()
    dec_copy = remote(dec.at[0], dec.at[1], scan_send.at[1], scan_recv.at[1], sibling)
    dec_copy.start()

    def convolve(first, count):
        for j in range(8):
            cols = slice(j * 128, (j + 1) * 128)
            if j < 4:
                taps = [xk_ref[k : k + 1, cols] for k in range(4)]
                offset = xo_ref[:, cols]
            else:
                start = (b_start if j < 6 else c_start) + (j % 2) * 128
                lanes = pl.ds(pl.multiple_of(start, 128), 128)
                taps = [bck_ref[k : k + 1, lanes] for k in range(4)]
                offset = bco_ref[:, lanes]
            acc = jnp.broadcast_to(offset, (count, 128))
            for k in range(4):
                acc = acc + taps[k] * raw[5 + k + first : 5 + k + first + count, cols]
            conv[first : first + count, cols] = (acc / (1.0 + jnp.exp(-acc))).astype(bf16)

    raw[8 : 8 + TOK, :] = xbc[...].astype(f32)
    convolve(16, TOK - 16)
    halo_copy.wait()
    not_first = (seq > 0).astype(f32)
    raw[0:8, :] = halo[...].astype(f32)[8:16, :] * not_first
    convolve(0, 16)

    dec_copy.wait()
    dec[2] = dec[0] * dec[1]
    decall[Y] = dec[2]
    dec_copies = []
    for k in range(1, NY):
        copy = remote(dec.at[2], decall.at[Y], scan_send.at[1 + k], scan_recv.at[2], y_at(k))
        copy.start()
        dec_copies.append(copy)

    x_conv = conv[:, 0:CH].astype(f32)
    weighted = (x_conv * end_weight).astype(bf16)
    own_state = dot(weighted, conv[:, CH : CH + N], ((0,), (0,)))
    state[...] = own_state
    statebf[...] = own_state.astype(bf16)
    sib_rows = pl.ds(pl.multiple_of(other * 256, 256), 256)
    own_rows = pl.ds(pl.multiple_of(C * 256, 256), 256)
    a_copy = remote(statebf.at[sib_rows], sibstate, scan_send.at[9], scan_recv.at[3], sibling)
    a_copy.start()

    b_conv = conv[:, CH : CH + N]
    c_conv = conv[:, CH + N : CH + 2 * N]
    inner = dot(c_conv, b_conv, ((1,), (1,)))

    def diagonal(h):
        gap = cum[:, h : h + 1] - rows[h : h + 1, :]
        mixing = jnp.exp(jnp.where(causal, gap, -jnp.inf)) * inner * rows[8 + h : 9 + h, :]
        lanes = slice(h * P_SIZE, (h + 1) * P_SIZE)
        ybase[:, lanes] = dot(mixing.astype(bf16), conv[:, lanes], ((1,), (0,)))

    diagonal(0)
    diagonal(1)

    def head_decay(ref, heads=4):
        return jnp.concatenate(
            [jnp.broadcast_to(ref[pl.ds(4 * C + i, 1), :], (P_SIZE, N)) for i in range(heads)], axis=0
        )

    a_copy.wait()
    first_core = (C == 0).astype(f32)
    own_half = state[own_rows, :]
    sib_half = sibstate[...].astype(f32)
    own_decay = head_decay(dec.at[0])
    sib_decay = head_decay(dec.at[1])
    total[...] = (
        own_half * (first_core * sib_decay + (1.0 - first_core))
        + sib_half * (first_core + (1.0 - first_core) * own_decay)
    ).astype(bf16)
    b_copies = []
    for k in range(1, NY):
        target = lax.rem(Y + k, NY)
        piece = pl.ds(pl.multiple_of(target * 32, 32), 32)
        copy = remote(total.at[piece], gath.at[Y], scan_send.at[9 + k], scan_recv.at[4], y_at(k))
        copy.start()
        b_copies.append(copy)
    gath[Y] = total[pl.ds(pl.multiple_of(Y * 32, 32), 32), :]

    for h in range(2, 8):
        diagonal(h)

    for copy in dec_copies + b_copies:
        copy.wait_send()
    arrived(decall.at[pl.ds(0, 7)], scan_recv.at[2])
    arrived(gath.at[pl.ds(0, 7)], scan_recv.at[4])
    my_head = 4 * C + Y // 2
    carried = jnp.zeros((32, N), f32)
    for k in range(NY):
        entout[k] = carried.astype(bf16)
        carried = decall[k, pl.ds(my_head, 1), :] * carried + gath[k].astype(f32)
    my_piece = pl.ds(pl.multiple_of(Y * 32, 32), 32)
    c_copies = []
    for k in range(1, NY):
        target = lax.rem(Y + k, NY)
        copy = remote(entout.at[target], entchip.at[my_piece], scan_send.at[16 + k], scan_recv.at[5], y_at(k))
        copy.start()
        c_copies.append(copy)
    entchip[my_piece, :] = entout[Y]

    skip = dot(dsk_ref[...], spread, ((1,), (0,)), HI)
    ybase[...] = ybase[...] + skip * x_conv
    grow = dot(jnp.exp(cum_cols), spread, ((1,), (0,)), HI)
    z_load.wait()

    for copy in c_copies:
        copy.wait_send()
    arrived(entchip.at[pl.ds(0, 224)], scan_recv.at[5])
    enter_first = entchip[...].astype(f32)
    enter_second = enter_first * (first_core * own_decay + (1.0 - first_core) * sib_decay) + (
        first_core * own_half + (1.0 - first_core) * sib_half
    )
    entsend[...] = (first_core * enter_second + (1.0 - first_core) * enter_first).astype(bf16)
    d_copy = remote(entsend, ent.at[own_rows], scan_send.at[24], scan_recv.at[6], sibling)
    d_copy.start()
    ent[own_rows, :] = (first_core * enter_first + (1.0 - first_core) * enter_second).astype(bf16)
    d_copy.wait()

    y_off = dot(c_conv, ent[...], ((1,), (1,)))
    zf = zb[...].astype(f32)
    gated = (ybase[...] + y_off * grow) * (zf / (1.0 + jnp.exp(-zf)))
    sq[0] = dot(jnp.ones((8, CH), f32), gated * gated, ((1,), (1,)), HI)
    in_group = lax.rem(Z, 4)
    sq_copies = []
    for k in range(1, 4):
        target = at(Y, C, X, Z - in_group + lax.rem(in_group + k, 4))
        copy = remote(sq.at[0], sq.at[k], scan_send.at[24 + k], scan_recv.at[6 + k], target)
        copy.start()
        sq_copies.append(copy)
    for copy in sq_copies:
        copy.wait()
    squares = sq[0] + sq[1] + sq[2] + sq[3]
    inv = lax.rsqrt(squares * (1.0 / 2048.0) + norm_eps)
    inv_cols = dot(inv, jnp.full((8, 128), 0.125, f32), ((0,), (0,)), HI)
    scale = jnp.concatenate([inv_cols] * 4, axis=1)
    own_tok = pl.ds(pl.multiple_of(C * TOK, TOK), TOK)
    slot_in[0, own_tok, :] = (gated * scale * gain_ref[...]).astype(bf16)

    def share_rows(side):
        return pl.ds(pl.multiple_of(C * 256 + side * 128, 128), 128)

    def sib_slot_rows(side):
        return pl.ds(pl.multiple_of(other * 256 + side * 128, 128), 128)

    right, left = y_at(1), y_at(NY - 1)

    def share(slot, side):
        return remote(
            slot_in.at[slot, share_rows(side)],
            slot_in.at[slot, share_rows(side)],
            c_send.at[slot, side],
            c_recv.at[slot, side],
            sibling,
        )

    def pass_on(slot, side, src_slot, src_side):
        return remote(
            slot_in.at[src_slot, share_rows(src_side)],
            slot_in.at[slot, share_rows(side)],
            y_send.at[slot, side],
            y_recv.at[slot, side],
            right if side == 0 else left,
        )

    for h in range(2):
        for side in range(2):
            pass_on(1 + h, side, 0, h).start()
        share(0, h).start()
    w_load.wait()

    def x_block(x):
        return pl.ds(pl.multiple_of(lax.rem(x + 2 * NX, NX) * 128, 128), 128)

    def x_long(slot, stage):
        src = part.at[slot, x_block(X + 2 * sigma)] if stage == 0 else xlong.at[slot, 0]
        return remote(src, xlong.at[slot, stage], x_send.at[slot, stage], x_recv.at[slot, stage], x_fwd)

    def x_short(slot):
        return remote(
            part.at[slot, x_block(X - sigma)], xshort.at[slot], x_send.at[slot, 2], x_recv.at[slot, 2], x_back
        )

    def z_copy(slot, k):
        target = lax.rem(Z + k, NZ)
        src = strip.at[slot, pl.ds(pl.multiple_of(target * 16, 16), 16)]
        return remote(src, zin.at[slot, k], z_send.at[slot, k], z_recv.at[slot, k], z_at(k))

    def final_rows(slot):
        half = lax.rem(slot + 1, 2)
        half = jnp.where(jnp.logical_or(slot == 0, slot == 7), lax.rem(X, 2), half)
        return pl.ds(pl.multiple_of(half * 128 + Z * 16, 16), 16)

    def final_y(slot):
        distance = (slot + 1) // 2
        return lax.rem(Y + NY + jnp.where(lax.rem(X, 2) == 0, -distance, distance), NY)

    def final_copy(slot, par):
        return remote(
            fin.at[slot, :, pl.ds(par * 256, 256)],
            out.at[final_rows(slot)],
            f_send.at[slot, par],
            f_recv.at[0],
            at(final_y(slot), owner_c, owner_x, owner_z + par),
        )

    def final_here(slot, par):
        return same(at(final_y(slot), owner_c, owner_x, owner_z + par), me)

    def step_of(t, carry):
        slot = t

        @pl.when(jnp.logical_and(t >= 1, t < SLOTS))
        def _():
            for side in range(2):
                pass_on(slot, side, slot, side).wait_recv()
                share(slot, side).start()

            @pl.when(t <= 4)
            def _():
                for side in range(2):
                    pass_on(slot + 2, side, slot, side).start()

            @pl.when(t == 5)
            def _():
                pass_on(7, 0, slot, 0).start()

            @pl.when(t == 6)
            def _():
                pass_on(7, 1, slot, 1).start()

        s1 = t - 1

        @pl.when(jnp.logical_and(t >= 1, t < SLOTS + 1))
        def _():
            x_long(s1, 0).wait_recv()
            xlong[s1, 0] = (
                xlong[s1, 0].astype(f32) + part[s1, x_block(X + sigma), :].astype(f32)
            ).astype(bf16)
            x_long(s1, 1).start()

        @pl.when(t < SLOTS)
        def _():
            for side in range(2):
                share(slot, side).wait_recv()
            part[slot] = dot(slot_in[slot], wb[...], ((1,), (0,))).astype(bf16)
            x_long(slot, 0).start()
            x_short(slot).start()

        s2 = t - 2

        @pl.when(jnp.logical_and(t >= 2, t < SLOTS + 2))
        def _():
            x_long(s2, 1).wait_recv()
            x_short(s2).wait_recv()
            strip[s2] = (
                xlong[s2, 1].astype(f32) + xshort[s2].astype(f32) + part[s2, x_block(X), :].astype(f32)
            ).astype(bf16)
            for k in range(1, NZ):
                z_copy(s2, k).start()

        s3 = t - 3

        @pl.when(t >= 3)
        def _():
            acc = strip[s3, pl.ds(pl.multiple_of(Z * 16, 16), 16), :].astype(f32)
            for k in range(1, NZ):
                z_copy(s3, k).wait_recv()
                acc = acc + zin[s3, k].astype(f32)
            fin[s3] = acc.astype(bf16)
            for par in range(2):
                here = final_here(s3, par)

                @pl.when(here)
                def _():
                    out[final_rows(s3), :] = fin[s3, :, par * 256 : (par + 1) * 256]

                @pl.when(jnp.logical_not(here))
                def _():
                    final_copy(s3, par).start()

        return carry

    lax.fori_loop(0, SLOTS + 3, step_of, 0)

    def drain(slot, carry):
        @pl.when(slot >= 1)
        def _():
            @pl.when(slot < 7)
            def _():
                for side in range(2):
                    pass_on(slot, side, slot, side).wait_send()

            @pl.when(slot == 7)
            def _():
                for side in range(2):
                    pass_on(7, side, 7, side).wait_send()

        for side in range(2):
            share(slot, side).wait_send()
        x_long(slot, 0).wait_send()
        x_long(slot, 1).wait_send()
        x_short(slot).wait_send()
        for k in range(1, NZ):
            z_copy(slot, k).wait_send()
        for par in range(2):

            @pl.when(jnp.logical_not(final_here(slot, par)))
            def _():
                final_copy(slot, par).wait_send()

        return carry

    lax.fori_loop(0, SLOTS, drain, 0)

    @pl.when(stays == 0)
    def _():
        arrived(out, f_recv.at[0])

    @pl.when(stays == 1)
    def _():
        arrived(out.at[pl.ds(0, TOK - 16)], f_recv.at[0])

    o_ref[...] = out[...]


def per_device(
    x_raw,
    bc_raw,
    z_raw,
    x_kernel,
    bc_kernel,
    x_offset,
    bc_offset,
    dt_raw,
    dt_bias,
    a_log,
    d_skip,
    norm_gain,
    out_weight,
):
    vmem = pl.BlockSpec(memory_space=pltpu.VMEM)
    hbm = pl.BlockSpec(memory_space=pl.ANY)
    V = pltpu.VMEM
    S = pltpu.SemaphoreType.DMA
    return pl.pallas_call(
        kernel,
        out_shape=jax.ShapeDtypeStruct((TOK, 256), bf16),
        in_specs=[hbm, hbm, hbm] + [vmem] * 9 + [hbm],
        out_specs=vmem,
        scratch_shapes=[
            V((TOK, 1024), bf16),
            V((TOK, CH), bf16),
            V((CH, CH), bf16),
            S((5,)),
            V((16, 1024), bf16),
            V((TOK + 8, 1024), f32),
            V((TOK, 1024), bf16),
            V((TOK, 8), f32),
            V((TOK, 8), f32),
            V((16, TOK), f32),
            V((TOK, CH), f32),
            V((CH, N), f32),
            V((CH, N), bf16),
            V((256, N), bf16),
            V((3, 8, 256), f32),
            V((8, 8, 256), f32),
            V((256, N), bf16),
            V((8, 32, N), bf16),
            V((8, 32, N), bf16),
            V((256, N), bf16),
            V((256, N), bf16),
            V((CH, N), bf16),
            V((4, 8, 256), f32),
            V((SLOTS, CH, CH), bf16),
            V((SLOTS, CH, CH), bf16),
            V((SLOTS, 2, 128, CH), bf16),
            V((SLOTS, 128, CH), bf16),
            V((SLOTS, 128, CH), bf16),
            V((SLOTS, 8, 16, CH), bf16),
            V((SLOTS, 16, CH), bf16),
            V((TOK, 256), bf16),
            S((28,)),
            S((10,)),
            S((SLOTS, 2)),
            S((SLOTS, 2)),
            S((SLOTS, 2)),
            S((SLOTS, 2)),
            S((SLOTS, 3)),
            S((SLOTS, 3)),
            S((SLOTS, 8)),
            S((SLOTS, 8)),
            S((SLOTS, 2)),
            S((1,)),
        ],
        compiler_params=pltpu.CompilerParams(
            collective_id=0, has_side_effects=True, vmem_limit_bytes=48 * 1024 * 1024
        ),
        name="mixer",
    )(
        x_raw,
        bc_raw,
        z_raw,
        x_kernel,
        bc_kernel,
        x_offset.reshape(1, -1),
        bc_offset.reshape(1, -1),
        dt_raw,
        dt_bias.reshape(1, -1),
        a_log.reshape(1, -1),
        d_skip.reshape(1, -1),
        norm_gain.reshape(1, -1),
        out_weight,
    )


def solution(mesh):
    return jax.shard_map(
        per_device,
        mesh=mesh,
        in_specs=(
            P("seq", "head"),
            P("seq", None),
            P("seq", "head"),
            P(None, "head"),
            P(),
            P("head"),
            P(),
            P("seq", "head"),
            P("head"),
            P("head"),
            P("head"),
            P("head"),
            P("head", "seq"),
        ),
        out_specs=P("seq", "head"),
        check_vma=False,
    )
```

```python
import jax
import jax.numpy as jnp
from jax import lax
from jax.experimental import pallas as pl
from jax.experimental.pallas import tpu as pltpu
from jax.sharding import PartitionSpec as P

P_SIZE = 64
N = 256
TOK = 256
CH = 512
HEADS_DEV = 8
NY, NX, NZ = 8, 4, 8
SLOTS = 8
RING_SLOTS = 4
RING_COLS = 256
LAG_LONG, LAG_STRIP, LAG_FINAL = 2, 4, 6
LAG_RING, LAG_RING_FINAL = 2, 10
STEPS = max(SLOTS + LAG_FINAL, RING_SLOTS + LAG_RING_FINAL)
norm_eps = 1e-05
MESH = pl.DeviceIdType.MESH
HI = lax.Precision.HIGHEST
f32 = jnp.float32
bf16 = jnp.bfloat16


def dot(a, b, dims, precision=None):
    return lax.dot_general(a, b, (dims, ((), ())), precision=precision, preferred_element_type=f32)


def kernel(
    x_hbm,
    bc_hbm,
    z_hbm,
    xk_hbm,
    bck_hbm,
    xo_hbm,
    bco_hbm,
    dt_hbm,
    dtb_hbm,
    alog_hbm,
    dsk_hbm,
    gain_hbm,
    w_hbm,
    o_ref,
    xbc,
    zb,
    wb,
    taps_ref,
    offsets,
    dt_ref,
    dtb_ref,
    alog_ref,
    dsk_ref,
    gain_ref,
    load_sem,
    halo,
    raw,
    conv,
    cum,
    rows,
    ybase,
    gate,
    state,
    statebf,
    sibstate,
    dec,
    decall,
    total,
    gath,
    entout,
    entchip,
    entsend,
    ent,
    sq,
    scales,
    slot_in,
    part,
    xin,
    strip,
    zin,
    fin,
    rlong,
    rshort,
    rstrip,
    rin,
    rfin,
    unused,
    out,
    scan_send,
    scan_recv,
    y_send,
    y_recv,
    x_send,
    x_recv,
    z_send,
    z_recv,
    r_send,
    r_recv,
    f_send,
    f_recv,
):
    seq = lax.axis_index("seq")
    head = lax.axis_index("head")
    Y, C = seq // 2, seq % 2
    X, Z = head // NZ, head % NZ
    group = head // 4
    other = 1 - C

    def at(y, c, x, z):
        return (y * 2 + c, x * NZ + z)

    b_start = pl.multiple_of(group * N, N)
    c_start = pl.multiple_of(8 * N + group * N, N)
    sources = [
        (x_hbm, xbc.at[:, pl.ds(0, CH)]),
        (bc_hbm.at[:, pl.ds(b_start, N)], xbc.at[:, pl.ds(CH, N)]),
        (bc_hbm.at[:, pl.ds(c_start, N)], xbc.at[:, pl.ds(CH + N, N)]),
        (dt_hbm, dt_ref),
        (dtb_hbm, dtb_ref),
        (alog_hbm, alog_ref),
        (xk_hbm, taps_ref.at[:, pl.ds(0, CH)]),
        (bck_hbm.at[:, pl.ds(b_start, N)], taps_ref.at[:, pl.ds(CH, N)]),
        (bck_hbm.at[:, pl.ds(c_start, N)], taps_ref.at[:, pl.ds(CH + N, N)]),
        (xo_hbm, offsets.at[:, pl.ds(0, CH)]),
        (bco_hbm.at[:, pl.ds(b_start, N)], offsets.at[:, pl.ds(CH, N)]),
        (bco_hbm.at[:, pl.ds(c_start, N)], offsets.at[:, pl.ds(CH + N, N)]),
        (dsk_hbm, dsk_ref),
        (gain_hbm, gain_ref),
        (z_hbm, zb),
        (w_hbm, wb.at[C]),
    ]
    loads = [pltpu.make_async_copy(src, dst, load_sem.at[i]) for i, (src, dst) in enumerate(sources)]
    for copy in loads:
        copy.start()

    sibling = at(Y, other, X, Z)
    after = (lax.rem(seq + 1, 16), head)
    cross = at(lax.rem(Y + NY - 1 + 2 * C, NY), other, X, Z)
    sigma = 1 - 2 * C
    x_fwd = at(Y, C, lax.rem(X + NX + sigma, NX), Z)
    x_back = at(Y, C, lax.rem(X + NX - sigma, NX), Z)

    def y_at(k):
        return at(lax.rem(Y + k, NY), C, X, Z)

    def x_at(k):
        return at(Y, C, lax.rem(X + k, NX), Z)

    def z_at(k):
        return at(Y, C, X, lax.rem(Z + k, NZ))

    owner_x = Y // 2
    owner_z = 4 * lax.rem(Y, 2)

    def same(a, b):
        return jnp.logical_and(a[0] == b[0], a[1] == b[1])

    me = (seq, head)

    barrier = pltpu.get_barrier_semaphore()

    def greet(device):
        pl.semaphore_signal(barrier, inc=1, device_id=device, device_id_type=MESH)

    greet(cross)
    greet(sibling)
    for k in range(1, NY):
        greet(y_at(k))
    for k in range(1, NZ):
        greet(z_at(k))
    for k in range(1, NX):
        greet(x_at(k))

    src_y = 2 * X + Z // 4
    src_half = lax.rem(Z // 2, 2)

    def greet_other(device):
        @pl.when(jnp.logical_not(same(device, me)))
        def _():
            greet(device)

    def greet_source(i, carry):
        greet_other(at(src_y, C, 2 * src_half + i // NZ, lax.rem(i, NZ)))
        return carry

    lax.fori_loop(0, 16, greet_source, 0)

    @pl.when(lax.rem(Z, 2) == 1)
    def _():
        def greet_ring_source(i, carry):
            greet_other(at(src_y, C, i // 4, 4 * src_half + lax.rem(i, 4)))
            return carry

        lax.fori_loop(0, 16, greet_ring_source, 0)

    stays = jnp.logical_and(owner_x == X, Z // 2 == (owner_z + 2 * (X // 2)) // 2)
    stays_ring = jnp.logical_and(owner_x == X, Z == owner_z + 2 * (Z // 4) + 1)
    greetings = 2 + (NY - 1) + (NZ - 1) + (NX - 1) + 24
    greetings = greetings - stays.astype(jnp.int32) - stays_ring.astype(jnp.int32)

    pos_t = lax.broadcasted_iota(jnp.int32, (TOK, TOK), 0)
    pos_s = lax.broadcasted_iota(jnp.int32, (TOK, TOK), 1)
    causal = pos_t >= pos_s
    eye = (pos_t == pos_s).astype(f32)
    eye8 = (
        lax.broadcasted_iota(jnp.int32, (8, 8), 0) == lax.broadcasted_iota(jnp.int32, (8, 8), 1)
    ).astype(f32)
    for copy in loads[3:6]:
        copy.wait()
    step_in = dot(dt_ref[...], eye8, ((0,), (0,)), HI) + dtb_ref[...]
    step = jnp.maximum(step_in, 0.0) + jnp.log1p(jnp.exp(-jnp.abs(step_in)))
    log_step = step * -jnp.exp(alog_ref[...])
    cum_cols = dot(causal.astype(f32), log_step, ((1,), (0,)), HI)
    cum[...] = cum_cols
    rows[0:8, :] = dot(cum_cols, eye, ((0,), (0,)), HI)
    rows[8:16, :] = dot(step, eye, ((0,), (0,)), HI)
    last_cols = cum_cols[TOK - 1 : TOK, :]
    dec[0] = jnp.broadcast_to(jnp.exp(rows[0:8, TOK - 1 : TOK]), (8, TOK))
    spread = (
        lax.broadcasted_iota(jnp.int32, (HEADS_DEV, CH), 1) // P_SIZE
        == lax.broadcasted_iota(jnp.int32, (HEADS_DEV, CH), 0)
    ).astype(f32)
    end_weight = dot(jnp.exp(last_cols - cum_cols) * step, spread, ((1,), (0,)), HI)

    for copy in loads[0:3] + loads[6:14]:
        copy.wait()
    raw[8 : 8 + TOK, :] = xbc[...].astype(f32)
    pl.semaphore_wait(barrier, greetings)

    def remote(src, dst, send, recv, device):
        return pltpu.make_async_remote_copy(
            src_ref=src, dst_ref=dst, send_sem=send, recv_sem=recv, device_id=device, device_id_type=MESH
        )

    def arrived(ref, sem):
        pltpu.make_async_copy(ref, ref, sem).wait()

    halo_copy = remote(xbc.at[pl.ds(TOK - 16, 16)], halo, scan_send.at[0], scan_recv.at[0], after)
    halo_copy.start()
    dec_copy = remote(dec.at[0], dec.at[1], scan_send.at[1], scan_recv.at[1], sibling)
    dec_copy.start()

    def convolve(first, count):
        for j in range(8):
            cols = slice(j * 128, (j + 1) * 128)
            acc = jnp.broadcast_to(offsets[:, cols], (count, 128))
            for k in range(4):
                acc = acc + taps_ref[k : k + 1, cols] * raw[5 + k + first : 5 + k + first + count, cols]
            conv[first : first + count, cols] = (acc / (1.0 + jnp.exp(-acc))).astype(bf16)

    convolve(16, TOK - 16)
    halo_copy.wait()
    not_first = (seq > 0).astype(f32)
    raw[0:8, :] = halo[...].astype(f32)[8:16, :] * not_first
    convolve(0, 16)

    x_conv = conv[:, 0:CH].astype(f32)
    weighted = (x_conv * end_weight).astype(bf16)
    own_state = dot(weighted, conv[:, CH : CH + N], ((0,), (0,)))
    state[...] = own_state
    statebf[...] = own_state.astype(bf16)
    sib_rows = pl.ds(pl.multiple_of(other * 256, 256), 256)
    own_rows = pl.ds(pl.multiple_of(C * 256, 256), 256)
    a_copy = remote(statebf.at[sib_rows], sibstate, scan_send.at[4], scan_recv.at[3], sibling)
    a_copy.start()

    dec_copy.wait()
    dec[2] = dec[0] * dec[1]
    for k in range(1, NY):
        remote(dec.at[2], decall.at[Y], scan_send.at[2], scan_recv.at[2], y_at(k)).start()
    decall[Y] = dec[2]

    b_conv = conv[:, CH : CH + N]
    c_conv = conv[:, CH + N : CH + 2 * N]
    inner = dot(c_conv, b_conv, ((1,), (1,)))

    def diagonal(h):
        gap = cum[:, h : h + 1] - rows[h : h + 1, :]
        mixing = jnp.exp(jnp.where(causal, gap, -jnp.inf)) * inner * rows[8 + h : 9 + h, :]
        lanes = slice(h * P_SIZE, (h + 1) * P_SIZE)
        ybase[:, lanes] = dot(mixing.astype(bf16), conv[:, lanes], ((1,), (0,)))

    def head_decay(ref):
        return jnp.concatenate(
            [jnp.broadcast_to(ref[pl.ds(4 * C + i, 1), :], (P_SIZE, N)) for i in range(4)], axis=0
        )

    first_core = (C == 0).astype(f32)
    a_copy.wait()
    total[...] = (
        state[own_rows, :] * (first_core * head_decay(dec.at[1]) + (1.0 - first_core))
        + sibstate[...].astype(f32) * (first_core + (1.0 - first_core) * head_decay(dec.at[0]))
    ).astype(bf16)
    for k in (4, 3, 5, 2, 6, 1, 7):
        target = lax.rem(Y + k, NY)
        piece = pl.ds(pl.multiple_of(target * 32, 32), 32)
        remote(total.at[piece], gath.at[Y], scan_send.at[3], scan_recv.at[4], y_at(k)).start()
    gath[Y] = total[pl.ds(pl.multiple_of(Y * 32, 32), 32), :]

    loads[15].wait()
    w_copy = remote(wb.at[C], wb.at[C], scan_send.at[8], scan_recv.at[8], sibling)
    w_copy.start()

    for h in range(8):
        diagonal(h)

    arrived(decall.at[pl.ds(0, 7)], scan_recv.at[2])
    arrived(gath.at[pl.ds(0, 7)], scan_recv.at[4])
    my_head = 4 * C + Y // 2
    carried = jnp.zeros((32, N), f32)
    for k in range(NY):
        entout[k] = carried.astype(bf16)
        carried = decall[k, pl.ds(my_head, 1), :] * carried + gath[k].astype(f32)
    my_piece = pl.ds(pl.multiple_of(Y * 32, 32), 32)
    for k in (4, 3, 5, 2, 6, 1, 7):
        target = lax.rem(Y + k, NY)
        remote(entout.at[target], entchip.at[my_piece], scan_send.at[5], scan_recv.at[5], y_at(k)).start()
    entchip[my_piece, :] = entout[Y]

    skip = dot(dsk_ref[...], spread, ((1,), (0,)), HI)
    loads[14].wait()
    zf = zb[...].astype(f32)
    silu_z = zf / (1.0 + jnp.exp(-zf))
    ybase[...] = (ybase[...] + skip * conv[:, 0:CH].astype(f32)) * silu_z
    gate[...] = silu_z * dot(jnp.exp(cum_cols), spread, ((1,), (0,)), HI)

    arrived(entchip.at[pl.ds(0, 224)], scan_recv.at[5])
    enter_first = entchip[...].astype(f32)
    enter_second = enter_first * (
        first_core * head_decay(dec.at[0]) + (1.0 - first_core) * head_decay(dec.at[1])
    ) + (first_core * state[own_rows, :] + (1.0 - first_core) * sibstate[...].astype(f32))
    entsend[...] = (first_core * enter_second + (1.0 - first_core) * enter_first).astype(bf16)
    d_copy = remote(entsend, ent.at[own_rows], scan_send.at[6], scan_recv.at[6], sibling)
    d_copy.start()
    ent[own_rows, :] = (first_core * enter_first + (1.0 - first_core) * enter_second).astype(bf16)
    d_copy.wait()

    y_off = dot(conv[:, CH + N : CH + 2 * N], ent[...], ((1,), (1,)))
    gated = ybase[...] + y_off * gate[...]
    slot_in[0] = (gated * gain_ref[...]).astype(bf16)

    def half_rows(side):
        return pl.ds(side * 128, 128)

    right, left = y_at(1), y_at(NY - 1)

    def pass_on(slot, side, src_slot, src_side):
        return remote(
            slot_in.at[src_slot, half_rows(src_side)],
            slot_in.at[slot, half_rows(side)],
            y_send.at[side],
            y_recv.at[slot, side],
            right if side == 0 else left,
        )

    for h in range(2):
        for side in range(2):
            pass_on(1 + h, side, 0, h).start()

    sq[0] = dot(jnp.ones((8, CH), f32), gated * gated, ((1,), (1,)), HI)
    in_group = lax.rem(Z, 4)
    for k in (3, 2, 1):
        target = at(Y, C, X, Z - in_group + lax.rem(in_group + k, 4))
        remote(sq.at[0], sq.at[k], scan_send.at[7], scan_recv.at[7], target).start()
    w_copy.wait()
    arrived(decall.at[pl.ds(0, 7)], scan_send.at[2])
    arrived(gath.at[pl.ds(0, 7)], scan_send.at[3])
    arrived(entchip.at[pl.ds(0, 224)], scan_send.at[5])
    arrived(sq.at[pl.ds(0, 3)], scan_recv.at[7])
    squares = sq[0] + sq[1] + sq[2] + sq[3]
    scales[Y] = lax.rsqrt(squares * (1.0 / 2048.0) + norm_eps)[0:1, :]
    for k in (4, 3, 5, 2, 6, 1, 7):
        remote(scales.at[Y], scales.at[Y], scan_send.at[9], scan_recv.at[9], y_at(k)).start()

    def scale_columns(slot, side):
        k = (slot + 1) // 2
        half = side if slot in (0, 7) else (slot + 1) % 2
        block = lax.rem(Y + NY + (k if side else -k), NY)
        row = jnp.broadcast_to(scales[block, :, half * 128 : half * 128 + 128], (8, 128))
        column = dot(row, jnp.full((8, 128), 0.125, f32), ((0,), (0,)), HI)
        return jnp.concatenate([column] * 4, axis=1)

    def width(slot):
        return pl.ds(0, CH - RING_COLS if slot < RING_SLOTS else CH)

    def x_block(x):
        return lax.rem(x + 2 * NX, NX)

    def x_long(slot, stage):
        cols = width(slot)
        src = part.at[slot, x_block(X + 2 * sigma), :, cols] if stage == 0 else xin.at[slot, 0, :, cols]
        return remote(src, xin.at[slot, stage, :, cols], x_send.at[slot], x_recv.at[slot, stage], x_fwd)

    def x_short(slot):
        cols = width(slot)
        return remote(
            part.at[slot, x_block(X - sigma), :, cols],
            xin.at[slot, 2, :, cols],
            x_send.at[slot],
            x_recv.at[slot, 1],
            x_back,
        )

    def z_copy(slot, k):
        target = lax.rem(Z + k, NZ)
        src = strip.at[slot, pl.ds(pl.multiple_of(target * 16, 16), 16), width(slot)]
        return remote(src, zin.at[slot, k - 1, :, width(slot)], z_send.at[slot], z_recv.at[slot], z_at(k))

    tail = pl.ds(CH - RING_COLS, RING_COLS)
    z_fwd, z_back = z_at(NZ + sigma), z_at(NZ - sigma)

    def z_block(slot, z):
        z = lax.rem(z + 2 * NZ, NZ)
        return part.at[slot, z // 2, pl.ds(pl.multiple_of(lax.rem(z, 2) * 64, 64), 64), tail]

    def ring_long(slot, stage):
        src = z_block(slot, Z + 4 * sigma) if stage == 0 else rlong.at[slot, stage - 1]
        return remote(src, rlong.at[slot, stage], r_send.at[slot, 0], r_recv.at[slot, stage], z_fwd)

    def ring_short(slot, stage):
        src = z_block(slot, Z - 3 * sigma) if stage == 0 else rshort.at[slot, stage - 1]
        return remote(src, rshort.at[slot, stage], r_send.at[slot, 1], r_recv.at[slot, 4 + stage], z_back)

    def ring_x(slot, k):
        target = lax.rem(X + k, NX)
        src = rstrip.at[slot, pl.ds(pl.multiple_of(target * 16, 16), 16)]
        return remote(src, rin.at[slot, k - 1], r_send.at[slot, 2], r_recv.at[slot, 7], x_at(k))

    def strip_row(slot, half, offset):
        if slot not in (0, 7):
            half = 1 - slot % 2
        return pl.ds(pl.multiple_of(half * 128 + offset, 16), 16)

    def strip_y(slot, side):
        distance = (slot + 1) // 2
        return lax.rem(Y + NY + jnp.where(side == 0, -distance, distance), NY)

    def hand_over(src, rows_to, cols_to, device):
        here = same(device, me)
        dst = out.at[rows_to, cols_to]

        @pl.when(here)
        def _():
            pltpu.make_async_copy(src, dst, f_recv.at[0]).start()
            pltpu.make_async_copy(src, unused.at[:, cols_to], f_send.at[0]).start()

        @pl.when(jnp.logical_not(here))
        def _():
            remote(src, dst, f_send.at[0], f_recv.at[0], device).start()

    def add(*values):
        acc = values[0].astype(f32)
        for value in values[1:]:
            acc = acc + value.astype(f32)
        return acc.astype(bf16)

    for t in range(STEPS):
        if 1 <= t < SLOTS:
            for side in range(2):
                pass_on(t, side, t, side).wait_recv()
                if t <= 4:
                    pass_on(t + 2, side, t, side).start()
                if t == 5 + side:
                    pass_on(7, side, t, side).start()

        if t < SLOTS:
            if t == 1:
                arrived(scales.at[pl.ds(0, 7)], scan_recv.at[9])
            scale = [scale_columns(t, side) for side in range(2)]
            for half in range(2):
                product = dot(slot_in[t], wb[half], ((1,), (0,)))
                for side in range(2):
                    part[t, 2 * half + side] = (product[side * 128 : side * 128 + 128] * scale[side]).astype(bf16)
            x_long(t, 0).start()
            x_short(t).start()
            if t < RING_SLOTS:
                ring_long(t, 0).start()
                ring_short(t, 0).start()

        slot = t - LAG_LONG
        if 0 <= slot < SLOTS:
            cols = width(slot)
            x_long(slot, 0).wait_recv()
            xin[slot, 0, :, cols] = add(xin[slot, 0, :, cols], part[slot, x_block(X + sigma), :, cols])
            x_long(slot, 1).start()

        for stage in range(1, 5):
            slot = t - stage * LAG_RING
            if not 0 <= slot < RING_SLOTS:
                continue
            ring_long(slot, stage - 1).wait_recv()
            if stage < 4:
                ring_short(slot, stage - 1).wait_recv()
                block = z_block(slot, Z + (4 - stage) * sigma)
                rlong[slot, stage - 1] = add(rlong[slot, stage - 1], block[...])
                ring_long(slot, stage).start()
            if stage < 3:
                block = z_block(slot, Z - (3 - stage) * sigma)
                rshort[slot, stage - 1] = add(rshort[slot, stage - 1], block[...])
                ring_short(slot, stage).start()
            if stage == 4:
                rstrip[slot] = add(rlong[slot, 3], rshort[slot, 2], z_block(slot, Z)[...])
                for k in (2, 1, 3):
                    ring_x(slot, k).start()

        slot = t - LAG_STRIP
        if 0 <= slot < SLOTS:
            cols = width(slot)
            arrived(xin.at[slot, pl.ds(1, 2), :, cols], x_recv.at[slot, 1])
            strip[slot, :, cols] = add(
                xin[slot, 1, :, cols], xin[slot, 2, :, cols], part[slot, X, :, cols]
            )
            for k in (4, 3, 5, 2, 6, 1, 7):
                z_copy(slot, k).start()

        slot = t - LAG_FINAL
        if 0 <= slot < SLOTS:
            cols = width(slot)
            arrived(zin.at[slot, :, :, cols], z_recv.at[slot])
            fin[slot, :, cols] = add(
                strip[slot, pl.ds(pl.multiple_of(Z * 16, 16), 16), cols],
                *[zin[slot, k, :, cols] for k in range(NZ - 1)],
            )
            side = lax.rem(X, 2)
            rows_to = strip_row(slot, side, Z * 16)
            y_to = strip_y(slot, side)
            z_to = owner_z + 2 * (X // 2)
            hand_over(fin.at[slot, :, pl.ds(0, 256)], rows_to, pl.ds(0, 256), at(y_to, C, owner_x, z_to))
            count = 256 - RING_COLS if slot < RING_SLOTS else 256
            hand_over(
                fin.at[slot, :, pl.ds(256, count)], rows_to, pl.ds(0, count), at(y_to, C, owner_x, z_to + 1)
            )

        slot = t - LAG_RING_FINAL
        if 0 <= slot < RING_SLOTS:
            arrived(rin.at[slot], r_recv.at[slot, 7])
            rfin[slot] = add(
                rstrip[slot, pl.ds(pl.multiple_of(X * 16, 16), 16), :], *[rin[slot, k] for k in range(NX - 1)]
            )
            side = lax.rem(Z // 2, 2)
            owner = at(strip_y(slot, side), C, owner_x, owner_z + 2 * (Z // 4) + 1)
            rows_to = strip_row(slot, side, lax.rem(Z, 2) * 64 + X * 16)
            hand_over(rfin.at[slot], rows_to, pl.ds(256 - RING_COLS, RING_COLS), owner)

    arrived(sq.at[pl.ds(0, 3)], scan_send.at[7])
    arrived(scales.at[pl.ds(0, 7)], scan_send.at[9])
    for side in range(2):
        arrived(slot_in.at[pl.ds(0, 7), pl.ds(0, 128)], y_send.at[side])
    for slot in range(SLOTS):
        arrived(xin.at[slot, :, :, width(slot)], x_send.at[slot])
        arrived(zin.at[slot, :, :, width(slot)], z_send.at[slot])
    for slot in range(RING_SLOTS):
        arrived(rlong.at[slot], r_send.at[slot, 0])
        arrived(rshort.at[slot], r_send.at[slot, 1])
        arrived(rin.at[slot], r_send.at[slot, 2])
    arrived(out, f_send.at[0])
    arrived(out, f_recv.at[0])

    o_ref[...] = out[...]


def per_device(
    x_raw,
    bc_raw,
    z_raw,
    x_kernel,
    bc_kernel,
    x_offset,
    bc_offset,
    dt_raw,
    dt_bias,
    a_log,
    d_skip,
    norm_gain,
    out_weight,
):
    hbm = pl.BlockSpec(memory_space=pltpu.HBM)
    V = pltpu.VMEM
    S = pltpu.SemaphoreType.DMA
    return pl.pallas_call(
        kernel,
        out_shape=jax.ShapeDtypeStruct((TOK, 256), bf16),
        in_specs=[hbm] * 13,
        out_specs=pl.BlockSpec(memory_space=pltpu.VMEM),
        scratch_shapes=[
            V((TOK, 1024), bf16),
            V((TOK, CH), bf16),
            V((2, CH, CH), bf16),
            V((4, 1024), f32),
            V((1, 1024), f32),
            V((8, TOK), f32),
            V((1, 8), f32),
            V((1, 8), f32),
            V((1, 8), f32),
            V((1, CH), f32),
            S((16,)),
            V((16, 1024), bf16),
            V((TOK + 8, 1024), f32),
            V((TOK, 1024), bf16),
            V((TOK, 8), f32),
            V((16, TOK), f32),
            V((TOK, CH), f32),
            V((TOK, CH), f32),
            V((CH, N), f32),
            V((CH, N), bf16),
            V((256, N), bf16),
            V((3, 8, 256), f32),
            V((8, 8, 256), f32),
            V((256, N), bf16),
            V((8, 32, N), bf16),
            V((8, 32, N), bf16),
            V((256, N), bf16),
            V((256, N), bf16),
            V((CH, N), bf16),
            V((4, 8, 256), f32),
            V((NY, 1, TOK), f32),
            V((SLOTS, TOK, CH), bf16),
            V((SLOTS, 4, 128, CH), bf16),
            V((SLOTS, 3, 128, CH), bf16),
            V((SLOTS, 128, CH), bf16),
            V((SLOTS, 7, 16, CH), bf16),
            V((SLOTS, 16, CH), bf16),
            V((RING_SLOTS, 4, 64, RING_COLS), bf16),
            V((RING_SLOTS, 3, 64, RING_COLS), bf16),
            V((RING_SLOTS, 64, RING_COLS), bf16),
            V((RING_SLOTS, 3, 16, RING_COLS), bf16),
            V((RING_SLOTS, 16, RING_COLS), bf16),
            V((16, 256), bf16),
            V((TOK, 256), bf16),
            S((10,)),
            S((10,)),
            S((2,)),
            S((SLOTS, 2)),
            S((SLOTS,)),
            S((SLOTS, 2)),
            S((SLOTS,)),
            S((SLOTS,)),
            S((RING_SLOTS, 3)),
            S((RING_SLOTS, 8)),
            S((1,)),
            S((1,)),
        ],
        compiler_params=pltpu.CompilerParams(
            collective_id=0, has_side_effects=True, vmem_limit_bytes=56 * 1024 * 1024
        ),
        name="mixer",
    )(
        x_raw,
        bc_raw,
        z_raw,
        x_kernel,
        bc_kernel,
        x_offset.reshape(1, -1),
        bc_offset.reshape(1, -1),
        dt_raw.T,
        dt_bias.reshape(1, -1),
        a_log.reshape(1, -1),
        d_skip.reshape(1, -1),
        norm_gain.reshape(1, -1),
        out_weight,
    )


def solution(mesh):
    return jax.shard_map(
        per_device,
        mesh=mesh,
        in_specs=(
            P("seq", "head"),
            P("seq", None),
            P("seq", "head"),
            P(None, "head"),
            P(),
            P("head"),
            P(),
            P("seq", "head"),
            P("head"),
            P("head"),
            P("head"),
            P("head"),
            P("head", "seq"),
        ),
        out_specs=P("seq", "head"),
        check_vma=False,
    )
```

```python
import jax
import jax.numpy as jnp
from jax import lax
from jax.experimental import pallas as pl
from jax.experimental.pallas import tpu as pltpu
from jax.sharding import PartitionSpec as P

P_SIZE = 64
N = 256
TOK = 256
CH = 512
HEADS_DEV = 8
NY, NX, NZ = 8, 4, 8
SLOTS = 8
RING_SLOTS = 5
RING_COLS = 256
LAG_LONG, LAG_STRIP, LAG_FINAL = 2, 4, 6
LAG_RING, LAG_RING_FINAL = 2, 10
STEPS = max(SLOTS + LAG_FINAL, RING_SLOTS + LAG_RING_FINAL)
norm_eps = 1e-05
MESH = pl.DeviceIdType.MESH
HI = lax.Precision.HIGHEST
f32 = jnp.float32
bf16 = jnp.bfloat16


def dot(a, b, dims, precision=None):
    return lax.dot_general(a, b, (dims, ((), ())), precision=precision, preferred_element_type=f32)


def kernel(
    x_hbm,
    bc_hbm,
    z_hbm,
    xk_hbm,
    bck_hbm,
    xo_hbm,
    bco_hbm,
    dt_hbm,
    dtb_hbm,
    alog_hbm,
    dsk_hbm,
    gain_hbm,
    w_hbm,
    o_ref,
    xbc,
    zb,
    wb,
    taps_ref,
    offsets,
    dt_ref,
    dtb_ref,
    alog_ref,
    dsk_ref,
    gain_ref,
    load_sem,
    halo,
    raw,
    conv,
    cum,
    rows,
    ybase,
    gate,
    state,
    statebf,
    sibstate,
    dec,
    decall,
    total,
    gath,
    entout,
    entchip,
    entsend,
    ent,
    sq,
    scales,
    slot_in,
    part,
    xin,
    strip,
    zin,
    fin,
    rlong,
    rshort,
    rstrip,
    rin,
    rfin,
    unused,
    out,
    scan_send,
    scan_recv,
    y_send,
    y_recv,
    x_send,
    x_recv,
    z_send,
    z_recv,
    r_send,
    r_recv,
    f_send,
    f_recv,
):
    seq = lax.axis_index("seq")
    head = lax.axis_index("head")
    Y, C = seq // 2, seq % 2
    X, Z = head // NZ, head % NZ
    group = head // 4
    other = 1 - C

    def at(y, c, x, z):
        return (y * 2 + c, x * NZ + z)

    b_start = pl.multiple_of(group * N, N)
    c_start = pl.multiple_of(8 * N + group * N, N)
    sources = [
        (x_hbm, xbc.at[:, pl.ds(0, CH)]),
        (bc_hbm.at[:, pl.ds(b_start, N)], xbc.at[:, pl.ds(CH, N)]),
        (bc_hbm.at[:, pl.ds(c_start, N)], xbc.at[:, pl.ds(CH + N, N)]),
        (dt_hbm, dt_ref),
        (dtb_hbm, dtb_ref),
        (alog_hbm, alog_ref),
        (xk_hbm, taps_ref.at[:, pl.ds(0, CH)]),
        (bck_hbm.at[:, pl.ds(b_start, N)], taps_ref.at[:, pl.ds(CH, N)]),
        (bck_hbm.at[:, pl.ds(c_start, N)], taps_ref.at[:, pl.ds(CH + N, N)]),
        (xo_hbm, offsets.at[:, pl.ds(0, CH)]),
        (bco_hbm.at[:, pl.ds(b_start, N)], offsets.at[:, pl.ds(CH, N)]),
        (bco_hbm.at[:, pl.ds(c_start, N)], offsets.at[:, pl.ds(CH + N, N)]),
        (dsk_hbm, dsk_ref),
        (gain_hbm, gain_ref),
        (z_hbm, zb),
        (w_hbm, wb.at[C]),
    ]
    loads = [pltpu.make_async_copy(src, dst, load_sem.at[i]) for i, (src, dst) in enumerate(sources)]
    for copy in loads:
        copy.start()

    sibling = at(Y, other, X, Z)
    after = (lax.rem(seq + 1, 16), head)
    cross = at(lax.rem(Y + NY - 1 + 2 * C, NY), other, X, Z)
    sigma = 1 - 2 * C
    x_fwd = at(Y, C, lax.rem(X + NX + sigma, NX), Z)
    x_back = at(Y, C, lax.rem(X + NX - sigma, NX), Z)

    def y_at(k):
        return at(lax.rem(Y + k, NY), C, X, Z)

    def x_at(k):
        return at(Y, C, lax.rem(X + k, NX), Z)

    def z_at(k):
        return at(Y, C, X, lax.rem(Z + k, NZ))

    owner_x = Y // 2
    owner_z = 4 * lax.rem(Y, 2)

    def same(a, b):
        return jnp.logical_and(a[0] == b[0], a[1] == b[1])

    me = (seq, head)

    barrier = pltpu.get_barrier_semaphore()

    def greet(device):
        pl.semaphore_signal(barrier, inc=1, device_id=device, device_id_type=MESH)

    greet(cross)
    greet(sibling)
    for k in range(1, NY):
        greet(y_at(k))
    for k in range(1, NZ):
        greet(z_at(k))
    for k in range(1, NX):
        greet(x_at(k))

    src_y = 2 * X + Z // 4
    src_half = lax.rem(Z // 2, 2)

    def greet_other(device):
        @pl.when(jnp.logical_not(same(device, me)))
        def _():
            greet(device)

    def greet_source(i, carry):
        greet_other(at(src_y, C, 2 * src_half + i // NZ, lax.rem(i, NZ)))
        return carry

    lax.fori_loop(0, 16, greet_source, 0)

    @pl.when(lax.rem(Z, 2) == 1)
    def _():
        def greet_ring_source(i, carry):
            greet_other(at(src_y, C, i // 4, 4 * src_half + lax.rem(i, 4)))
            return carry

        lax.fori_loop(0, 16, greet_ring_source, 0)

    stays = jnp.logical_and(owner_x == X, Z // 2 == (owner_z + 2 * (X // 2)) // 2)
    stays_ring = jnp.logical_and(owner_x == X, Z == owner_z + 2 * (Z // 4) + 1)
    greetings = 2 + (NY - 1) + (NZ - 1) + (NX - 1) + 24
    greetings = greetings - stays.astype(jnp.int32) - stays_ring.astype(jnp.int32)

    pos_t = lax.broadcasted_iota(jnp.int32, (TOK, TOK), 0)
    pos_s = lax.broadcasted_iota(jnp.int32, (TOK, TOK), 1)
    causal = pos_t >= pos_s
    eye = (pos_t == pos_s).astype(f32)
    eye8 = (
        lax.broadcasted_iota(jnp.int32, (8, 8), 0) == lax.broadcasted_iota(jnp.int32, (8, 8), 1)
    ).astype(f32)
    for copy in loads[3:6]:
        copy.wait()
    step_in = dot(dt_ref[...], eye8, ((0,), (0,)), HI) + dtb_ref[...]
    step = jnp.maximum(step_in, 0.0) + jnp.log1p(jnp.exp(-jnp.abs(step_in)))
    log_step = step * -jnp.exp(alog_ref[...])
    cum_cols = dot(causal.astype(f32), log_step, ((1,), (0,)), HI)
    cum[...] = cum_cols
    rows[0:8, :] = dot(cum_cols, eye, ((0,), (0,)), HI)
    rows[8:16, :] = dot(step, eye, ((0,), (0,)), HI)
    last_cols = cum_cols[TOK - 1 : TOK, :]
    dec[0] = jnp.broadcast_to(jnp.exp(rows[0:8, TOK - 1 : TOK]), (8, TOK))
    spread = (
        lax.broadcasted_iota(jnp.int32, (HEADS_DEV, CH), 1) // P_SIZE
        == lax.broadcasted_iota(jnp.int32, (HEADS_DEV, CH), 0)
    ).astype(f32)
    end_weight = dot(jnp.exp(last_cols - cum_cols) * step, spread, ((1,), (0,)), HI)

    for copy in loads[0:3] + loads[6:14]:
        copy.wait()
    raw[8 : 8 + TOK, :] = xbc[...].astype(f32)
    def convolve(first, count):
        for j in range(8):
            cols = slice(j * 128, (j + 1) * 128)
            acc = jnp.broadcast_to(offsets[:, cols], (count, 128))
            for k in range(4):
                acc = acc + taps_ref[k : k + 1, cols] * raw[5 + k + first : 5 + k + first + count, cols]
            conv[first : first + count, cols] = (acc / (1.0 + jnp.exp(-acc))).astype(bf16)

    convolve(16, TOK - 16)

    def state_of(first, count):
        pick = slice(first, first + count)
        weighted = (conv[pick, 0:CH].astype(f32) * end_weight[pick, :]).astype(bf16)
        return dot(weighted, conv[pick, CH : CH + N], ((0,), (0,)))

    state[...] = state_of(16, TOK - 16)
    pl.semaphore_wait(barrier, greetings)

    def remote(src, dst, send, recv, device):
        return pltpu.make_async_remote_copy(
            src_ref=src, dst_ref=dst, send_sem=send, recv_sem=recv, device_id=device, device_id_type=MESH
        )

    def arrived(ref, sem):
        pltpu.make_async_copy(ref, ref, sem).wait()

    halo_copy = remote(xbc.at[pl.ds(TOK - 16, 16)], halo, scan_send.at[0], scan_recv.at[0], after)
    halo_copy.start()
    dec_copy = remote(dec.at[0], dec.at[1], scan_send.at[1], scan_recv.at[1], sibling)
    dec_copy.start()

    halo_copy.wait()
    not_first = (seq > 0).astype(f32)
    raw[0:8, :] = halo[...].astype(f32)[8:16, :] * not_first
    convolve(0, 16)

    own_state = state[...] + state_of(0, 16)
    state[...] = own_state
    statebf[...] = own_state.astype(bf16)
    sib_rows = pl.ds(pl.multiple_of(other * 256, 256), 256)
    own_rows = pl.ds(pl.multiple_of(C * 256, 256), 256)
    a_copy = remote(statebf.at[sib_rows], sibstate, scan_send.at[4], scan_recv.at[3], sibling)
    a_copy.start()

    dec_copy.wait()
    dec[2] = dec[0] * dec[1]
    for k in range(1, NY):
        remote(dec.at[2], decall.at[Y], scan_send.at[2], scan_recv.at[2], y_at(k)).start()
    decall[Y] = dec[2]

    b_conv = conv[:, CH : CH + N]
    c_conv = conv[:, CH + N : CH + 2 * N]
    inner = dot(c_conv, b_conv, ((1,), (1,)))

    def diagonal(h):
        gap = cum[:, h : h + 1] - rows[h : h + 1, :]
        mixing = jnp.exp(jnp.where(causal, gap, -jnp.inf)) * inner * rows[8 + h : 9 + h, :]
        lanes = slice(h * P_SIZE, (h + 1) * P_SIZE)
        ybase[:, lanes] = dot(mixing.astype(bf16), conv[:, lanes], ((1,), (0,)))

    def head_decay(ref):
        return jnp.concatenate(
            [jnp.broadcast_to(ref[pl.ds(4 * C + i, 1), :], (P_SIZE, N)) for i in range(4)], axis=0
        )

    first_core = (C == 0).astype(f32)
    a_copy.wait()
    total[...] = (
        state[own_rows, :] * (first_core * head_decay(dec.at[1]) + (1.0 - first_core))
        + sibstate[...].astype(f32) * (first_core + (1.0 - first_core) * head_decay(dec.at[0]))
    ).astype(bf16)
    for k in (4, 3, 5, 2, 6, 1, 7):
        target = lax.rem(Y + k, NY)
        piece = pl.ds(pl.multiple_of(target * 32, 32), 32)
        remote(total.at[piece], gath.at[Y], scan_send.at[3], scan_recv.at[4], y_at(k)).start()
    gath[Y] = total[pl.ds(pl.multiple_of(Y * 32, 32), 32), :]

    loads[15].wait()
    w_copy = remote(wb.at[C], wb.at[C], scan_send.at[8], scan_recv.at[8], sibling)
    w_copy.start()

    for h in range(8):
        diagonal(h)

    arrived(decall.at[pl.ds(0, 7)], scan_recv.at[2])
    arrived(gath.at[pl.ds(0, 7)], scan_recv.at[4])
    my_head = 4 * C + Y // 2
    carried = jnp.zeros((32, N), f32)
    for k in range(NY):
        entout[k] = carried.astype(bf16)
        carried = decall[k, pl.ds(my_head, 1), :] * carried + gath[k].astype(f32)
    my_piece = pl.ds(pl.multiple_of(Y * 32, 32), 32)
    for k in (4, 3, 5, 2, 6, 1, 7):
        target = lax.rem(Y + k, NY)
        remote(entout.at[target], entchip.at[my_piece], scan_send.at[5], scan_recv.at[5], y_at(k)).start()
    entchip[my_piece, :] = entout[Y]

    skip = dot(dsk_ref[...], spread, ((1,), (0,)), HI)
    loads[14].wait()
    zf = zb[...].astype(f32)
    silu_z = zf / (1.0 + jnp.exp(-zf))
    ybase[...] = (ybase[...] + skip * conv[:, 0:CH].astype(f32)) * silu_z
    gate[...] = silu_z * dot(jnp.exp(cum_cols), spread, ((1,), (0,)), HI)

    arrived(entchip.at[pl.ds(0, 224)], scan_recv.at[5])
    enter_first = entchip[...].astype(f32)
    enter_second = enter_first * (
        first_core * head_decay(dec.at[0]) + (1.0 - first_core) * head_decay(dec.at[1])
    ) + (first_core * state[own_rows, :] + (1.0 - first_core) * sibstate[...].astype(f32))
    entsend[...] = (first_core * enter_second + (1.0 - first_core) * enter_first).astype(bf16)
    d_copy = remote(entsend, ent.at[own_rows], scan_send.at[6], scan_recv.at[6], sibling)
    d_copy.start()
    ent[own_rows, :] = (first_core * enter_first + (1.0 - first_core) * enter_second).astype(bf16)
    d_copy.wait()

    y_off = dot(conv[:, CH + N : CH + 2 * N], ent[...], ((1,), (1,)))
    gated = ybase[...] + y_off * gate[...]
    slot_in[0] = (gated * gain_ref[...]).astype(bf16)

    def half_rows(side):
        return pl.ds(side * 128, 128)

    right, left = y_at(1), y_at(NY - 1)

    def pass_on(slot, side, src_slot, src_side):
        return remote(
            slot_in.at[src_slot, half_rows(src_side)],
            slot_in.at[slot, half_rows(side)],
            y_send.at[side],
            y_recv.at[slot, side],
            right if side == 0 else left,
        )

    for h in range(2):
        for side in range(2):
            pass_on(1 + h, side, 0, h).start()

    squared = gated * gated
    folded = squared[:, 0:128] + squared[:, 128:256] + squared[:, 256:384] + squared[:, 384:512]
    sq[0] = dot(jnp.ones((8, 128), f32), folded, ((1,), (1,)), HI)
    in_group = lax.rem(Z, 4)
    for k in (3, 2, 1):
        target = at(Y, C, X, Z - in_group + lax.rem(in_group + k, 4))
        remote(sq.at[0], sq.at[k], scan_send.at[7], scan_recv.at[7], target).start()
    w_copy.wait()
    first_products = [dot(slot_in[0], wb[half], ((1,), (0,))) for half in range(2)]
    arrived(decall.at[pl.ds(0, 7)], scan_send.at[2])
    arrived(gath.at[pl.ds(0, 7)], scan_send.at[3])
    arrived(entchip.at[pl.ds(0, 224)], scan_send.at[5])
    arrived(sq.at[pl.ds(0, 3)], scan_recv.at[7])
    squares = sq[0] + sq[1] + sq[2] + sq[3]
    scales[Y] = lax.rsqrt(squares * (1.0 / 2048.0) + norm_eps)[0:1, :]
    for k in (1, 7, 2, 6, 3, 5, 4):
        distance = min(k, NY - k)
        remote(scales.at[Y], scales.at[Y], scan_send.at[9], scan_recv.at[8 + distance], y_at(k)).start()

    def scale_columns(slot, side):
        k = (slot + 1) // 2
        half = side if slot in (0, 7) else (slot + 1) % 2
        block = lax.rem(Y + NY + (k if side else -k), NY)
        row = jnp.broadcast_to(scales[block, :, half * 128 : half * 128 + 128], (8, 128))
        column = dot(row, jnp.full((8, 128), 0.125, f32), ((0,), (0,)), HI)
        return jnp.concatenate([column] * 4, axis=1)

    def width(slot):
        return pl.ds(0, CH - RING_COLS if slot < RING_SLOTS else CH)

    def x_block(x):
        return lax.rem(x + 2 * NX, NX)

    def x_long(slot, stage):
        cols = width(slot)
        src = part.at[slot, x_block(X + 2 * sigma), :, cols] if stage == 0 else xin.at[slot, 0, :, cols]
        return remote(src, xin.at[slot, stage, :, cols], x_send.at[slot], x_recv.at[slot, stage], x_fwd)

    def x_short(slot):
        cols = width(slot)
        return remote(
            part.at[slot, x_block(X - sigma), :, cols],
            xin.at[slot, 2, :, cols],
            x_send.at[slot],
            x_recv.at[slot, 1],
            x_back,
        )

    def z_copy(slot, k):
        target = lax.rem(Z + k, NZ)
        src = strip.at[slot, pl.ds(pl.multiple_of(target * 16, 16), 16), width(slot)]
        return remote(src, zin.at[slot, k - 1, :, width(slot)], z_send.at[slot], z_recv.at[slot], z_at(k))

    tail = pl.ds(CH - RING_COLS, RING_COLS)
    z_fwd, z_back = z_at(NZ + sigma), z_at(NZ - sigma)

    def z_block(slot, z):
        z = lax.rem(z + 2 * NZ, NZ)
        return part.at[slot, z // 2, pl.ds(pl.multiple_of(lax.rem(z, 2) * 64, 64), 64), tail]

    def ring_long(slot, stage):
        src = z_block(slot, Z + 4 * sigma) if stage == 0 else rlong.at[slot, stage - 1]
        return remote(src, rlong.at[slot, stage], r_send.at[slot, 0], r_recv.at[slot, stage], z_fwd)

    def ring_short(slot, stage):
        src = z_block(slot, Z - 3 * sigma) if stage == 0 else rshort.at[slot, stage - 1]
        return remote(src, rshort.at[slot, stage], r_send.at[slot, 1], r_recv.at[slot, 4 + stage], z_back)

    def ring_x(slot, k):
        target = lax.rem(X + k, NX)
        src = rstrip.at[slot, pl.ds(pl.multiple_of(target * 16, 16), 16)]
        return remote(src, rin.at[slot, k - 1], r_send.at[slot, 2], r_recv.at[slot, 7], x_at(k))

    def strip_row(slot, half, offset):
        if slot not in (0, 7):
            half = 1 - slot % 2
        return pl.ds(pl.multiple_of(half * 128 + offset, 16), 16)

    def strip_y(slot, side):
        distance = (slot + 1) // 2
        return lax.rem(Y + NY + jnp.where(side == 0, -distance, distance), NY)

    def hand_over(src, rows_to, cols_to, device):
        here = same(device, me)
        dst = out.at[rows_to, cols_to]

        @pl.when(here)
        def _():
            pltpu.make_async_copy(src, dst, f_recv.at[0]).start()
            pltpu.make_async_copy(src, unused.at[:, cols_to], f_send.at[0]).start()

        @pl.when(jnp.logical_not(here))
        def _():
            remote(src, dst, f_send.at[0], f_recv.at[0], device).start()

    def add(*values):
        acc = values[0].astype(f32)
        for value in values[1:]:
            acc = acc + value.astype(f32)
        return acc.astype(bf16)

    for t in range(STEPS):
        if 1 <= t < SLOTS:
            for side in range(2):
                pass_on(t, side, t, side).wait_recv()
                if t <= 4:
                    pass_on(t + 2, side, t, side).start()
                if t == 5 + side:
                    pass_on(7, side, t, side).start()

        if t < SLOTS:
            if t % 2 == 1:
                arrived(scales.at[pl.ds(0, 2 if t < 7 else 1)], scan_recv.at[9 + t // 2])
            scale = [scale_columns(t, side) for side in range(2)]
            for half in range(2):
                product = first_products[half] if t == 0 else dot(slot_in[t], wb[half], ((1,), (0,)))
                for side in range(2):
                    part[t, 2 * half + side] = (product[side * 128 : side * 128 + 128] * scale[side]).astype(bf16)
            x_long(t, 0).start()
            x_short(t).start()
            if t < RING_SLOTS:
                ring_long(t, 0).start()
                ring_short(t, 0).start()

        slot = t - LAG_LONG
        if 0 <= slot < SLOTS:
            cols = width(slot)
            x_long(slot, 0).wait_recv()
            xin[slot, 0, :, cols] = add(xin[slot, 0, :, cols], part[slot, x_block(X + sigma), :, cols])
            x_long(slot, 1).start()

        for stage in range(1, 5):
            slot = t - stage * LAG_RING
            if not 0 <= slot < RING_SLOTS:
                continue
            ring_long(slot, stage - 1).wait_recv()
            if stage < 4:
                ring_short(slot, stage - 1).wait_recv()
                block = z_block(slot, Z + (4 - stage) * sigma)
                rlong[slot, stage - 1] = add(rlong[slot, stage - 1], block[...])
                ring_long(slot, stage).start()
            if stage < 3:
                block = z_block(slot, Z - (3 - stage) * sigma)
                rshort[slot, stage - 1] = add(rshort[slot, stage - 1], block[...])
                ring_short(slot, stage).start()
            if stage == 4:
                rstrip[slot] = add(rlong[slot, 3], rshort[slot, 2], z_block(slot, Z)[...])
                for k in (2, 1, 3):
                    ring_x(slot, k).start()

        slot = t - LAG_STRIP
        if 0 <= slot < SLOTS:
            cols = width(slot)
            arrived(xin.at[slot, pl.ds(1, 2), :, cols], x_recv.at[slot, 1])
            strip[slot, :, cols] = add(
                xin[slot, 1, :, cols], xin[slot, 2, :, cols], part[slot, X, :, cols]
            )
            for k in (4, 3, 5, 2, 6, 1, 7):
                z_copy(slot, k).start()

        slot = t - LAG_FINAL
        if 0 <= slot < SLOTS:
            cols = width(slot)
            arrived(zin.at[slot, :, :, cols], z_recv.at[slot])
            fin[slot, :, cols] = add(
                strip[slot, pl.ds(pl.multiple_of(Z * 16, 16), 16), cols],
                *[zin[slot, k, :, cols] for k in range(NZ - 1)],
            )
            side = lax.rem(X, 2)
            rows_to = strip_row(slot, side, Z * 16)
            y_to = strip_y(slot, side)
            z_to = owner_z + 2 * (X // 2)
            hand_over(fin.at[slot, :, pl.ds(0, 256)], rows_to, pl.ds(0, 256), at(y_to, C, owner_x, z_to))
            count = 256 - RING_COLS if slot < RING_SLOTS else 256
            hand_over(
                fin.at[slot, :, pl.ds(256, count)], rows_to, pl.ds(0, count), at(y_to, C, owner_x, z_to + 1)
            )

        slot = t - LAG_RING_FINAL
        if 0 <= slot < RING_SLOTS:
            arrived(rin.at[slot], r_recv.at[slot, 7])
            rfin[slot] = add(
                rstrip[slot, pl.ds(pl.multiple_of(X * 16, 16), 16), :], *[rin[slot, k] for k in range(NX - 1)]
            )
            side = lax.rem(Z // 2, 2)
            owner = at(strip_y(slot, side), C, owner_x, owner_z + 2 * (Z // 4) + 1)
            rows_to = strip_row(slot, side, lax.rem(Z, 2) * 64 + X * 16)
            hand_over(rfin.at[slot], rows_to, pl.ds(256 - RING_COLS, RING_COLS), owner)

    arrived(sq.at[pl.ds(0, 3)], scan_send.at[7])
    arrived(scales.at[pl.ds(0, 7)], scan_send.at[9])
    for side in range(2):
        arrived(slot_in.at[pl.ds(0, 7), pl.ds(0, 128)], y_send.at[side])
    for slot in range(SLOTS):
        arrived(xin.at[slot, :, :, width(slot)], x_send.at[slot])
        arrived(zin.at[slot, :, :, width(slot)], z_send.at[slot])
    for slot in range(RING_SLOTS):
        arrived(rlong.at[slot], r_send.at[slot, 0])
        arrived(rshort.at[slot], r_send.at[slot, 1])
        arrived(rin.at[slot], r_send.at[slot, 2])
    arrived(out, f_send.at[0])
    arrived(out, f_recv.at[0])

    o_ref[...] = out[...]


def per_device(
    x_raw,
    bc_raw,
    z_raw,
    x_kernel,
    bc_kernel,
    x_offset,
    bc_offset,
    dt_raw,
    dt_bias,
    a_log,
    d_skip,
    norm_gain,
    out_weight,
):
    hbm = pl.BlockSpec(memory_space=pltpu.HBM)
    V = pltpu.VMEM
    S = pltpu.SemaphoreType.DMA
    return pl.pallas_call(
        kernel,
        out_shape=jax.ShapeDtypeStruct((TOK, 256), bf16),
        in_specs=[hbm] * 13,
        out_specs=pl.BlockSpec(memory_space=pltpu.VMEM),
        scratch_shapes=[
            V((TOK, 1024), bf16),
            V((TOK, CH), bf16),
            V((2, CH, CH), bf16),
            V((4, 1024), f32),
            V((1, 1024), f32),
            V((8, TOK), f32),
            V((1, 8), f32),
            V((1, 8), f32),
            V((1, 8), f32),
            V((1, CH), f32),
            S((16,)),
            V((16, 1024), bf16),
            V((TOK + 8, 1024), f32),
            V((TOK, 1024), bf16),
            V((TOK, 8), f32),
            V((16, TOK), f32),
            V((TOK, CH), f32),
            V((TOK, CH), f32),
            V((CH, N), f32),
            V((CH, N), bf16),
            V((256, N), bf16),
            V((3, 8, 256), f32),
            V((8, 8, 256), f32),
            V((256, N), bf16),
            V((8, 32, N), bf16),
            V((8, 32, N), bf16),
            V((256, N), bf16),
            V((256, N), bf16),
            V((CH, N), bf16),
            V((4, 8, 256), f32),
            V((NY, 1, TOK), f32),
            V((SLOTS, TOK, CH), bf16),
            V((SLOTS, 4, 128, CH), bf16),
            V((SLOTS, 3, 128, CH), bf16),
            V((SLOTS, 128, CH), bf16),
            V((SLOTS, 7, 16, CH), bf16),
            V((SLOTS, 16, CH), bf16),
            V((RING_SLOTS, 4, 64, RING_COLS), bf16),
            V((RING_SLOTS, 3, 64, RING_COLS), bf16),
            V((RING_SLOTS, 64, RING_COLS), bf16),
            V((RING_SLOTS, 3, 16, RING_COLS), bf16),
            V((RING_SLOTS, 16, RING_COLS), bf16),
            V((16, 256), bf16),
            V((TOK, 256), bf16),
            S((10,)),
            S((13,)),
            S((2,)),
            S((SLOTS, 2)),
            S((SLOTS,)),
            S((SLOTS, 2)),
            S((SLOTS,)),
            S((SLOTS,)),
            S((RING_SLOTS, 3)),
            S((RING_SLOTS, 8)),
            S((1,)),
            S((1,)),
        ],
        compiler_params=pltpu.CompilerParams(
            collective_id=0, has_side_effects=True, vmem_limit_bytes=56 * 1024 * 1024
        ),
        name="mixer",
    )(
        x_raw,
        bc_raw,
        z_raw,
        x_kernel,
        bc_kernel,
        x_offset.reshape(1, -1),
        bc_offset.reshape(1, -1),
        dt_raw.T,
        dt_bias.reshape(1, -1),
        a_log.reshape(1, -1),
        d_skip.reshape(1, -1),
        norm_gain.reshape(1, -1),
        out_weight,
    )


def solution(mesh):
    return jax.shard_map(
        per_device,
        mesh=mesh,
        in_specs=(
            P("seq", "head"),
            P("seq", None),
            P("seq", "head"),
            P(None, "head"),
            P(),
            P("head"),
            P(),
            P("seq", "head"),
            P("head"),
            P("head"),
            P("head"),
            P("head"),
            P("head", "seq"),
        ),
        out_specs=P("seq", "head"),
        check_vma=False,
    )
```

```python
import jax
import jax.numpy as jnp
from jax import lax
from jax.experimental import pallas as pl
from jax.experimental.pallas import tpu as pltpu
from jax.sharding import PartitionSpec as P

P_SIZE = 64
N = 256
TOK = 256
CH = 512
HEADS_DEV = 8
NY, NX, NZ = 8, 4, 8
SLOTS = 8
RING_SLOTS = 5
RING_COLS = 256
LAG_LONG, LAG_STRIP, LAG_FINAL = 2, 4, 6
LAG_RING, LAG_RING_FINAL = 2, 10
STEPS = max(SLOTS + LAG_FINAL, RING_SLOTS + LAG_RING_FINAL)
norm_eps = 1e-05
MESH = pl.DeviceIdType.MESH
HI = lax.Precision.HIGHEST
f32 = jnp.float32
bf16 = jnp.bfloat16


def dot(a, b, dims, precision=None):
    return lax.dot_general(a, b, (dims, ((), ())), precision=precision, preferred_element_type=f32)


def kernel(
    x_hbm,
    bc_hbm,
    z_hbm,
    xk_hbm,
    bck_hbm,
    xo_hbm,
    bco_hbm,
    dt_hbm,
    dtb_hbm,
    alog_hbm,
    dsk_hbm,
    gain_hbm,
    w_hbm,
    o_ref,
    xbc,
    zb,
    wb,
    taps_ref,
    offsets,
    dt_ref,
    dtb_ref,
    alog_ref,
    dsk_ref,
    gain_ref,
    load_sem,
    halo,
    raw,
    conv,
    cum,
    rows,
    ybase,
    gate,
    state,
    statebf,
    sibstate,
    dec,
    decall,
    total,
    gath,
    entout,
    entchip,
    entsend,
    ent,
    sq,
    scales,
    slot_in,
    part,
    xin,
    strip,
    zin,
    fin,
    rlong,
    rshort,
    rstrip,
    rin,
    rfin,
    unused,
    out,
    scan_send,
    scan_recv,
    y_send,
    y_recv,
    x_send,
    x_recv,
    z_send,
    z_recv,
    r_send,
    r_recv,
    f_send,
    f_recv,
):
    seq = lax.axis_index("seq")
    head = lax.axis_index("head")
    Y, C = seq // 2, seq % 2
    X, Z = head // NZ, head % NZ
    group = head // 4
    other = 1 - C

    def at(y, c, x, z):
        return (y * 2 + c, x * NZ + z)

    b_start = pl.multiple_of(group * N, N)
    c_start = pl.multiple_of(8 * N + group * N, N)
    sources = [
        (x_hbm, xbc.at[:, pl.ds(0, CH)]),
        (bc_hbm.at[:, pl.ds(b_start, N)], xbc.at[:, pl.ds(CH, N)]),
        (bc_hbm.at[:, pl.ds(c_start, N)], xbc.at[:, pl.ds(CH + N, N)]),
        (dt_hbm, dt_ref),
        (dtb_hbm, dtb_ref),
        (alog_hbm, alog_ref),
        (xk_hbm, taps_ref.at[:, pl.ds(0, CH)]),
        (bck_hbm.at[:, pl.ds(b_start, N)], taps_ref.at[:, pl.ds(CH, N)]),
        (bck_hbm.at[:, pl.ds(c_start, N)], taps_ref.at[:, pl.ds(CH + N, N)]),
        (xo_hbm, offsets.at[:, pl.ds(0, CH)]),
        (bco_hbm.at[:, pl.ds(b_start, N)], offsets.at[:, pl.ds(CH, N)]),
        (bco_hbm.at[:, pl.ds(c_start, N)], offsets.at[:, pl.ds(CH + N, N)]),
        (dsk_hbm, dsk_ref),
        (gain_hbm, gain_ref),
        (z_hbm, zb),
        (w_hbm, wb.at[C]),
    ]
    loads = [pltpu.make_async_copy(src, dst, load_sem.at[i]) for i, (src, dst) in enumerate(sources)]
    for copy in loads:
        copy.start()

    sibling = at(Y, other, X, Z)
    after = (lax.rem(seq + 1, 16), head)
    cross = at(lax.rem(Y + NY - 1 + 2 * C, NY), other, X, Z)
    sigma = 1 - 2 * C
    x_fwd = at(Y, C, lax.rem(X + NX + sigma, NX), Z)
    x_back = at(Y, C, lax.rem(X + NX - sigma, NX), Z)

    def y_at(k):
        return at(lax.rem(Y + k, NY), C, X, Z)

    def x_at(k):
        return at(Y, C, lax.rem(X + k, NX), Z)

    def z_at(k):
        return at(Y, C, X, lax.rem(Z + k, NZ))

    owner_x = Y // 2
    owner_z = 4 * lax.rem(Y, 2)

    def same(a, b):
        return jnp.logical_and(a[0] == b[0], a[1] == b[1])

    me = (seq, head)

    barrier = pltpu.get_barrier_semaphore()

    def greet(device):
        pl.semaphore_signal(barrier, inc=1, device_id=device, device_id_type=MESH)

    src_y = 2 * X + Z // 4
    src_half = lax.rem(Z // 2, 2)

    def greet_other(device):
        @pl.when(jnp.logical_not(same(device, me)))
        def _():
            greet(device)

    def greet_source(i, carry):
        greet_other(at(src_y, C, 2 * src_half + i // NZ, lax.rem(i, NZ)))
        return carry

    lax.fori_loop(0, 16, greet_source, 0)

    @pl.when(lax.rem(Z, 2) == 1)
    def _():
        def greet_ring_source(i, carry):
            greet_other(at(src_y, C, i // 4, 4 * src_half + lax.rem(i, 4)))
            return carry

        lax.fori_loop(0, 16, greet_ring_source, 0)

    for k in (4, 3, 5, 2, 6, 1, 7):
        greet(z_at(k))
    for k in (4, 3, 5, 2, 6, 1, 7):
        greet(y_at(k))
    for k in range(1, NX):
        greet(x_at(k))
    greet(cross)
    greet(sibling)

    stays = jnp.logical_and(owner_x == X, Z // 2 == (owner_z + 2 * (X // 2)) // 2)
    stays_ring = jnp.logical_and(owner_x == X, Z == owner_z + 2 * (Z // 4) + 1)
    greetings = 2 + (NY - 1) + (NZ - 1) + (NX - 1) + 24
    greetings = greetings - stays.astype(jnp.int32) - stays_ring.astype(jnp.int32)

    pos_t = lax.broadcasted_iota(jnp.int32, (TOK, TOK), 0)
    pos_s = lax.broadcasted_iota(jnp.int32, (TOK, TOK), 1)
    causal = pos_t >= pos_s
    eye = (pos_t == pos_s).astype(f32)
    eye8 = (
        lax.broadcasted_iota(jnp.int32, (8, 8), 0) == lax.broadcasted_iota(jnp.int32, (8, 8), 1)
    ).astype(f32)
    for copy in loads[3:6]:
        copy.wait()
    step_in = dot(dt_ref[...], eye8, ((0,), (0,)), HI) + dtb_ref[...]
    step = jnp.maximum(step_in, 0.0) + jnp.log1p(jnp.exp(-jnp.abs(step_in)))
    log_step = step * -jnp.exp(alog_ref[...])
    cum_cols = dot(causal.astype(f32), log_step, ((1,), (0,)), HI)
    cum[...] = cum_cols
    rows[0:8, :] = dot(cum_cols, eye, ((0,), (0,)), HI)
    rows[8:16, :] = dot(step, eye, ((0,), (0,)), HI)
    last_cols = cum_cols[TOK - 1 : TOK, :]
    dec[0] = jnp.broadcast_to(jnp.exp(rows[0:8, TOK - 1 : TOK]), (8, TOK))
    spread = (
        lax.broadcasted_iota(jnp.int32, (HEADS_DEV, CH), 1) // P_SIZE
        == lax.broadcasted_iota(jnp.int32, (HEADS_DEV, CH), 0)
    ).astype(f32)
    end_weight = dot(jnp.exp(last_cols - cum_cols) * step, spread, ((1,), (0,)), HI)

    for copy in loads[0:3] + loads[6:14]:
        copy.wait()
    raw[8 : 8 + TOK, :] = xbc[...].astype(f32)
    def convolve(first, count):
        for j in range(8):
            cols = slice(j * 128, (j + 1) * 128)
            acc = jnp.broadcast_to(offsets[:, cols], (count, 128))
            for k in range(4):
                acc = acc + taps_ref[k : k + 1, cols] * raw[5 + k + first : 5 + k + first + count, cols]
            conv[first : first + count, cols] = (acc / (1.0 + jnp.exp(-acc))).astype(bf16)

    convolve(16, TOK - 16)

    def state_of(first, count):
        pick = slice(first, first + count)
        weighted = (conv[pick, 0:CH].astype(f32) * end_weight[pick, :]).astype(bf16)
        return dot(weighted, conv[pick, CH : CH + N], ((0,), (0,)))

    state[...] = state_of(16, TOK - 16)
    pl.semaphore_wait(barrier, greetings)

    def remote(src, dst, send, recv, device):
        return pltpu.make_async_remote_copy(
            src_ref=src, dst_ref=dst, send_sem=send, recv_sem=recv, device_id=device, device_id_type=MESH
        )

    def arrived(ref, sem):
        pltpu.make_async_copy(ref, ref, sem).wait()

    halo_copy = remote(xbc.at[pl.ds(TOK - 16, 16)], halo, scan_send.at[0], scan_recv.at[0], after)
    halo_copy.start()
    dec_copy = remote(dec.at[0], dec.at[1], scan_send.at[1], scan_recv.at[1], sibling)
    dec_copy.start()

    halo_copy.wait()
    not_first = (seq > 0).astype(f32)
    raw[0:8, :] = halo[...].astype(f32)[8:16, :] * not_first
    convolve(0, 16)

    own_state = state[...] + state_of(0, 16)
    state[...] = own_state
    statebf[...] = own_state.astype(bf16)
    sib_rows = pl.ds(pl.multiple_of(other * 256, 256), 256)
    own_rows = pl.ds(pl.multiple_of(C * 256, 256), 256)
    a_copy = remote(statebf.at[sib_rows], sibstate, scan_send.at[4], scan_recv.at[3], sibling)
    a_copy.start()

    dec_copy.wait()
    dec[2] = dec[0] * dec[1]
    for k in range(1, NY):
        remote(dec.at[2], decall.at[Y], scan_send.at[2], scan_recv.at[2], y_at(k)).start()
    decall[Y] = dec[2]

    b_conv = conv[:, CH : CH + N]
    c_conv = conv[:, CH + N : CH + 2 * N]
    inner = dot(c_conv, b_conv, ((1,), (1,)))

    def diagonal(h):
        gap = cum[:, h : h + 1] - rows[h : h + 1, :]
        mixing = jnp.exp(jnp.where(causal, gap, -jnp.inf)) * inner * rows[8 + h : 9 + h, :]
        lanes = slice(h * P_SIZE, (h + 1) * P_SIZE)
        ybase[:, lanes] = dot(mixing.astype(bf16), conv[:, lanes], ((1,), (0,)))

    def head_decay(ref):
        return jnp.concatenate(
            [jnp.broadcast_to(ref[pl.ds(4 * C + i, 1), :], (P_SIZE, N)) for i in range(4)], axis=0
        )

    first_core = (C == 0).astype(f32)
    a_copy.wait()
    total[...] = (
        state[own_rows, :] * (first_core * head_decay(dec.at[1]) + (1.0 - first_core))
        + sibstate[...].astype(f32) * (first_core + (1.0 - first_core) * head_decay(dec.at[0]))
    ).astype(bf16)
    for k in (4, 3, 5, 2, 6, 1, 7):
        target = lax.rem(Y + k, NY)
        piece = pl.ds(pl.multiple_of(target * 32, 32), 32)
        remote(total.at[piece], gath.at[Y], scan_send.at[3], scan_recv.at[4], y_at(k)).start()
    gath[Y] = total[pl.ds(pl.multiple_of(Y * 32, 32), 32), :]

    loads[15].wait()
    w_copy = remote(wb.at[C], wb.at[C], scan_send.at[8], scan_recv.at[8], sibling)
    w_copy.start()

    for h in range(8):
        diagonal(h)

    arrived(decall.at[pl.ds(0, 7)], scan_recv.at[2])
    arrived(gath.at[pl.ds(0, 7)], scan_recv.at[4])
    my_head = 4 * C + Y // 2
    carried = jnp.zeros((32, N), f32)
    for k in range(NY):
        entout[k] = carried.astype(bf16)
        carried = decall[k, pl.ds(my_head, 1), :] * carried + gath[k].astype(f32)
    my_piece = pl.ds(pl.multiple_of(Y * 32, 32), 32)
    for k in (4, 3, 5, 2, 6, 1, 7):
        target = lax.rem(Y + k, NY)
        remote(entout.at[target], entchip.at[my_piece], scan_send.at[5], scan_recv.at[5], y_at(k)).start()
    entchip[my_piece, :] = entout[Y]

    skip = dot(dsk_ref[...], spread, ((1,), (0,)), HI)
    loads[14].wait()
    zf = zb[...].astype(f32)
    silu_z = zf / (1.0 + jnp.exp(-zf))
    ybase[...] = (ybase[...] + skip * conv[:, 0:CH].astype(f32)) * silu_z
    gate[...] = silu_z * dot(jnp.exp(cum_cols), spread, ((1,), (0,)), HI)

    arrived(entchip.at[pl.ds(0, 224)], scan_recv.at[5])
    enter_first = entchip[...].astype(f32)
    enter_second = enter_first * (
        first_core * head_decay(dec.at[0]) + (1.0 - first_core) * head_decay(dec.at[1])
    ) + (first_core * state[own_rows, :] + (1.0 - first_core) * sibstate[...].astype(f32))
    entsend[...] = (first_core * enter_second + (1.0 - first_core) * enter_first).astype(bf16)
    d_copy = remote(entsend, ent.at[own_rows], scan_send.at[6], scan_recv.at[6], sibling)
    d_copy.start()
    ent[own_rows, :] = (first_core * enter_first + (1.0 - first_core) * enter_second).astype(bf16)
    d_copy.wait()

    y_off = dot(conv[:, CH + N : CH + 2 * N], ent[...], ((1,), (1,)))
    gated = ybase[...] + y_off * gate[...]
    slot_in[0] = (gated * gain_ref[...]).astype(bf16)

    def half_rows(side):
        return pl.ds(side * 128, 128)

    right, left = y_at(1), y_at(NY - 1)

    def pass_on(slot, side, src_slot, src_side):
        return remote(
            slot_in.at[src_slot, half_rows(src_side)],
            slot_in.at[slot, half_rows(side)],
            y_send.at[side],
            y_recv.at[slot, side],
            right if side == 0 else left,
        )

    for h in range(2):
        for side in range(2):
            pass_on(1 + h, side, 0, h).start()

    squared = gated * gated
    folded = squared[:, 0:128] + squared[:, 128:256] + squared[:, 256:384] + squared[:, 384:512]
    sq[0] = dot(jnp.ones((8, 128), f32), folded, ((1,), (1,)), HI)
    in_group = lax.rem(Z, 4)
    for k in (3, 2, 1):
        target = at(Y, C, X, Z - in_group + lax.rem(in_group + k, 4))
        remote(sq.at[0], sq.at[k], scan_send.at[7], scan_recv.at[7], target).start()
    w_copy.wait()
    first_products = [dot(slot_in[0], wb[half], ((1,), (0,))) for half in range(2)]
    arrived(decall.at[pl.ds(0, 7)], scan_send.at[2])
    arrived(gath.at[pl.ds(0, 7)], scan_send.at[3])
    arrived(entchip.at[pl.ds(0, 224)], scan_send.at[5])
    arrived(sq.at[pl.ds(0, 3)], scan_recv.at[7])
    squares = sq[0] + sq[1] + sq[2] + sq[3]
    scales[Y] = lax.rsqrt(squares * (1.0 / 2048.0) + norm_eps)[0:1, :]
    for k in (1, 7, 2, 6, 3, 5, 4):
        distance = min(k, NY - k)
        remote(scales.at[Y], scales.at[Y], scan_send.at[9], scan_recv.at[8 + distance], y_at(k)).start()

    def scale_columns(slot, side):
        k = (slot + 1) // 2
        half = side if slot in (0, 7) else (slot + 1) % 2
        block = lax.rem(Y + NY + (k if side else -k), NY)
        row = jnp.broadcast_to(scales[block, :, half * 128 : half * 128 + 128], (8, 128))
        column = dot(row, jnp.full((8, 128), 0.125, f32), ((0,), (0,)), HI)
        return jnp.concatenate([column] * 4, axis=1)

    def width(slot):
        return pl.ds(0, CH - RING_COLS if slot < RING_SLOTS else CH)

    def x_block(x):
        return lax.rem(x + 2 * NX, NX)

    def x_long(slot, stage):
        cols = width(slot)
        src = part.at[slot, x_block(X + 2 * sigma), :, cols] if stage == 0 else xin.at[slot, 0, :, cols]
        return remote(src, xin.at[slot, stage, :, cols], x_send.at[slot], x_recv.at[slot, stage], x_fwd)

    def x_short(slot):
        cols = width(slot)
        return remote(
            part.at[slot, x_block(X - sigma), :, cols],
            xin.at[slot, 2, :, cols],
            x_send.at[slot],
            x_recv.at[slot, 1],
            x_back,
        )

    def z_copy(slot, k):
        target = lax.rem(Z + k, NZ)
        src = strip.at[slot, pl.ds(pl.multiple_of(target * 16, 16), 16), width(slot)]
        return remote(src, zin.at[slot, k - 1, :, width(slot)], z_send.at[slot], z_recv.at[slot], z_at(k))

    tail = pl.ds(CH - RING_COLS, RING_COLS)
    z_fwd, z_back = z_at(NZ + sigma), z_at(NZ - sigma)

    def z_block(slot, z):
        z = lax.rem(z + 2 * NZ, NZ)
        return part.at[slot, z // 2, pl.ds(pl.multiple_of(lax.rem(z, 2) * 64, 64), 64), tail]

    def ring_long(slot, stage):
        src = z_block(slot, Z + 4 * sigma) if stage == 0 else rlong.at[slot, stage - 1]
        return remote(src, rlong.at[slot, stage], r_send.at[slot, 0], r_recv.at[slot, stage], z_fwd)

    def ring_short(slot, stage):
        src = z_block(slot, Z - 3 * sigma) if stage == 0 else rshort.at[slot, stage - 1]
        return remote(src, rshort.at[slot, stage], r_send.at[slot, 1], r_recv.at[slot, 4 + stage], z_back)

    def ring_x(slot, k):
        target = lax.rem(X + k, NX)
        src = rstrip.at[slot, pl.ds(pl.multiple_of(target * 16, 16), 16)]
        return remote(src, rin.at[slot, k - 1], r_send.at[slot, 2], r_recv.at[slot, 7], x_at(k))

    def strip_row(slot, half, offset):
        if slot not in (0, 7):
            half = 1 - slot % 2
        return pl.ds(pl.multiple_of(half * 128 + offset, 16), 16)

    def strip_y(slot, side):
        distance = (slot + 1) // 2
        return lax.rem(Y + NY + jnp.where(side == 0, -distance, distance), NY)

    def hand_over(src, rows_to, cols_to, device):
        here = same(device, me)
        dst = out.at[rows_to, cols_to]

        @pl.when(here)
        def _():
            pltpu.make_async_copy(src, dst, f_recv.at[0]).start()
            pltpu.make_async_copy(src, unused.at[:, cols_to], f_send.at[0]).start()

        @pl.when(jnp.logical_not(here))
        def _():
            remote(src, dst, f_send.at[0], f_recv.at[0], device).start()

    def add(*values):
        acc = values[0].astype(f32)
        for value in values[1:]:
            acc = acc + value.astype(f32)
        return acc.astype(bf16)

    for t in range(STEPS):
        if 1 <= t < SLOTS:
            for side in range(2):
                pass_on(t, side, t, side).wait_recv()
                if t <= 4:
                    pass_on(t + 2, side, t, side).start()
                if t == 5 + side:
                    pass_on(7, side, t, side).start()

        if t < SLOTS:
            if t % 2 == 1:
                arrived(scales.at[pl.ds(0, 2 if t < 7 else 1)], scan_recv.at[9 + t // 2])
            scale = [scale_columns(t, side) for side in range(2)]
            for half in range(2):
                product = first_products[half] if t == 0 else dot(slot_in[t], wb[half], ((1,), (0,)))
                for side in range(2):
                    part[t, 2 * half + side] = (product[side * 128 : side * 128 + 128] * scale[side]).astype(bf16)
            x_long(t, 0).start()
            x_short(t).start()
            if t < RING_SLOTS:
                ring_long(t, 0).start()
                ring_short(t, 0).start()

        slot = t - LAG_LONG
        if 0 <= slot < SLOTS:
            cols = width(slot)
            x_long(slot, 0).wait_recv()
            xin[slot, 0, :, cols] = add(xin[slot, 0, :, cols], part[slot, x_block(X + sigma), :, cols])
            x_long(slot, 1).start()

        for stage in range(1, 5):
            slot = t - stage * LAG_RING
            if not 0 <= slot < RING_SLOTS:
                continue
            ring_long(slot, stage - 1).wait_recv()
            if stage < 4:
                ring_short(slot, stage - 1).wait_recv()
                block = z_block(slot, Z + (4 - stage) * sigma)
                rlong[slot, stage - 1] = add(rlong[slot, stage - 1], block[...])
                ring_long(slot, stage).start()
            if stage < 3:
                block = z_block(slot, Z - (3 - stage) * sigma)
                rshort[slot, stage - 1] = add(rshort[slot, stage - 1], block[...])
                ring_short(slot, stage).start()
            if stage == 4:
                rstrip[slot] = add(rlong[slot, 3], rshort[slot, 2], z_block(slot, Z)[...])
                for k in (2, 1, 3):
                    ring_x(slot, k).start()

        slot = t - LAG_STRIP
        if 0 <= slot < SLOTS:
            cols = width(slot)
            arrived(xin.at[slot, pl.ds(1, 2), :, cols], x_recv.at[slot, 1])
            strip[slot, :, cols] = add(
                xin[slot, 1, :, cols], xin[slot, 2, :, cols], part[slot, X, :, cols]
            )
            for k in (4, 3, 5, 2, 6, 1, 7):
                z_copy(slot, k).start()

        slot = t - LAG_FINAL
        if 0 <= slot < SLOTS:
            cols = width(slot)
            arrived(zin.at[slot, :, :, cols], z_recv.at[slot])
            fin[slot, :, cols] = add(
                strip[slot, pl.ds(pl.multiple_of(Z * 16, 16), 16), cols],
                *[zin[slot, k, :, cols] for k in range(NZ - 1)],
            )
            side = lax.rem(X, 2)
            rows_to = strip_row(slot, side, Z * 16)
            y_to = strip_y(slot, side)
            z_to = owner_z + 2 * (X // 2)
            hand_over(fin.at[slot, :, pl.ds(0, 256)], rows_to, pl.ds(0, 256), at(y_to, C, owner_x, z_to))
            count = 256 - RING_COLS if slot < RING_SLOTS else 256
            hand_over(
                fin.at[slot, :, pl.ds(256, count)], rows_to, pl.ds(0, count), at(y_to, C, owner_x, z_to + 1)
            )

        slot = t - LAG_RING_FINAL
        if 0 <= slot < RING_SLOTS:
            arrived(rin.at[slot], r_recv.at[slot, 7])
            rfin[slot] = add(
                rstrip[slot, pl.ds(pl.multiple_of(X * 16, 16), 16), :], *[rin[slot, k] for k in range(NX - 1)]
            )
            side = lax.rem(Z // 2, 2)
            owner = at(strip_y(slot, side), C, owner_x, owner_z + 2 * (Z // 4) + 1)
            rows_to = strip_row(slot, side, lax.rem(Z, 2) * 64 + X * 16)
            hand_over(rfin.at[slot], rows_to, pl.ds(256 - RING_COLS, RING_COLS), owner)

    arrived(sq.at[pl.ds(0, 3)], scan_send.at[7])
    arrived(scales.at[pl.ds(0, 7)], scan_send.at[9])
    for side in range(2):
        arrived(slot_in.at[pl.ds(0, 7), pl.ds(0, 128)], y_send.at[side])
    for slot in range(SLOTS):
        arrived(xin.at[slot, :, :, width(slot)], x_send.at[slot])
        arrived(zin.at[slot, :, :, width(slot)], z_send.at[slot])
    for slot in range(RING_SLOTS):
        arrived(rlong.at[slot], r_send.at[slot, 0])
        arrived(rshort.at[slot], r_send.at[slot, 1])
        arrived(rin.at[slot], r_send.at[slot, 2])
    arrived(out, f_send.at[0])
    arrived(out, f_recv.at[0])

    o_ref[...] = out[...]


def per_device(
    x_raw,
    bc_raw,
    z_raw,
    x_kernel,
    bc_kernel,
    x_offset,
    bc_offset,
    dt_raw,
    dt_bias,
    a_log,
    d_skip,
    norm_gain,
    out_weight,
):
    hbm = pl.BlockSpec(memory_space=pltpu.HBM)
    V = pltpu.VMEM
    S = pltpu.SemaphoreType.DMA
    return pl.pallas_call(
        kernel,
        out_shape=jax.ShapeDtypeStruct((TOK, 256), bf16),
        in_specs=[hbm] * 13,
        out_specs=pl.BlockSpec(memory_space=pltpu.VMEM),
        scratch_shapes=[
            V((TOK, 1024), bf16),
            V((TOK, CH), bf16),
            V((2, CH, CH), bf16),
            V((4, 1024), f32),
            V((1, 1024), f32),
            V((8, TOK), f32),
            V((1, 8), f32),
            V((1, 8), f32),
            V((1, 8), f32),
            V((1, CH), f32),
            S((16,)),
            V((16, 1024), bf16),
            V((TOK + 8, 1024), f32),
            V((TOK, 1024), bf16),
            V((TOK, 8), f32),
            V((16, TOK), f32),
            V((TOK, CH), f32),
            V((TOK, CH), f32),
            V((CH, N), f32),
            V((CH, N), bf16),
            V((256, N), bf16),
            V((3, 8, 256), f32),
            V((8, 8, 256), f32),
            V((256, N), bf16),
            V((8, 32, N), bf16),
            V((8, 32, N), bf16),
            V((256, N), bf16),
            V((256, N), bf16),
            V((CH, N), bf16),
            V((4, 8, 256), f32),
            V((NY, 1, TOK), f32),
            V((SLOTS, TOK, CH), bf16),
            V((SLOTS, 4, 128, CH), bf16),
            V((SLOTS, 3, 128, CH), bf16),
            V((SLOTS, 128, CH), bf16),
            V((SLOTS, 7, 16, CH), bf16),
            V((SLOTS, 16, CH), bf16),
            V((RING_SLOTS, 4, 64, RING_COLS), bf16),
            V((RING_SLOTS, 3, 64, RING_COLS), bf16),
            V((RING_SLOTS, 64, RING_COLS), bf16),
            V((RING_SLOTS, 3, 16, RING_COLS), bf16),
            V((RING_SLOTS, 16, RING_COLS), bf16),
            V((16, 256), bf16),
            V((TOK, 256), bf16),
            S((10,)),
            S((13,)),
            S((2,)),
            S((SLOTS, 2)),
            S((SLOTS,)),
            S((SLOTS, 2)),
            S((SLOTS,)),
            S((SLOTS,)),
            S((RING_SLOTS, 3)),
            S((RING_SLOTS, 8)),
            S((1,)),
            S((1,)),
        ],
        compiler_params=pltpu.CompilerParams(
            collective_id=0, has_side_effects=True, vmem_limit_bytes=56 * 1024 * 1024
        ),
        name="mixer",
    )(
        x_raw,
        bc_raw,
        z_raw,
        x_kernel,
        bc_kernel,
        x_offset.reshape(1, -1),
        bc_offset.reshape(1, -1),
        dt_raw.T,
        dt_bias.reshape(1, -1),
        a_log.reshape(1, -1),
        d_skip.reshape(1, -1),
        norm_gain.reshape(1, -1),
        out_weight,
    )


def solution(mesh):
    return jax.shard_map(
        per_device,
        mesh=mesh,
        in_specs=(
            P("seq", "head"),
            P("seq", None),
            P("seq", "head"),
            P(None, "head"),
            P(),
            P("head"),
            P(),
            P("seq", "head"),
            P("head"),
            P("head"),
            P("head"),
            P("head"),
            P("head", "seq"),
        ),
        out_specs=P("seq", "head"),
        check_vma=False,
    )
```
